256 devices in a mesh: dp: 32 (over z, x), head: 8 (over y, core).
Axes of the slice: x: 4, y: 4, z: 8, core: 2. Of those that a mesh axis runs over, the one named last changes fastest.
Arguments:
- query_in: bfloat16 [32, 1024, 4096], P(None, 'dp', 'head'), may hold values from -36 to 36
- key_in: bfloat16 [32, 1024, 1024], P(None, 'dp', 'head'), may hold values from -36 to 36
- value_input: bfloat16 [32, 1024, 1024], P(None, 'dp', 'head'), may hold values from -6 to 6
- grad_out: bfloat16 [32, 1024, 4096], P(None, 'dp', 'head'), may hold values from -16 to 16
- q_gain: float32 [128], replicated, may hold values from 0.5 to 7
- k_gain: float32 [128], replicated, may hold values from 0.5 to 7
- lengths: int32 [32], replicated, may hold values from 512 to 1024
- owners: int32 [32], replicated, may hold values from 0 to 31, as said below
- doc_ids: int32 [32, 1024], replicated, may hold values from 0 to 7, never falling along the last dimension, each value on 1 to 512 neighbouring positions
Outputs:
- attention: bfloat16 [32, 1024, 4096], P('dp', 'head')
- query_gradient_packed: bfloat16 [32, 1024, 4096], P('dp', 'head')
- key_gradient_packed: bfloat16 [32, 1024, 1024], P('dp', 'head')
- value_grad: bfloat16 [32, 1024, 1024], P('dp', 'head')
- q_gain_grad: float32 [128], replicated
- key_gain_gradient: float32 [128], replicated
The draws below stay inside these ranges and needn't reach their ends.
Inputs may be any that keep to these rules, and one draw needn't show every extreme that they name: `owners`: each of the 32 data shards owns exactly 1 sequence.
All inputs are finite; a program needn't handle non-finite values.
Results may differ from the reference program's by a relative error of at most 0.0075.
The reference program's roundings to bfloat16 on the way count: a program that leaves them out, or rounds other values in their place, can miss the bound.
Values may be sent and summed in bfloat16 or wider, within the bound.
No kernel may reach another device: no remote copies, remote signals or barrier semaphores. Data moves between devices by JAX's collectives and lax.ppermute only.
A program may use at most 64 MiB of HBM per device.

```python
import math
import jax
import jax.numpy as jnp
import numpy as np
from jax import lax

QUERY_HEADS = 32
KEY_VALUE_HEADS = 8
HEAD_WIDTH = 128
SLOT_LENGTH = 1024
SEQ_DEV = 1
DOCS = 8
SEQUENCE_COUNT = 32


def owner_list(key):
    key = jax.random.fold_in(key, 101)
    shuffled = jax.random.permutation(key, SEQUENCE_COUNT)
    return (shuffled // SEQ_DEV).astype(jnp.int32)


def gained_block(key, salt, heads, row_low, row_high):
    key = jax.random.fold_in(key, salt)
    first_key = jax.random.fold_in(key, 0)
    third_key = jax.random.fold_in(key, 2)
    fourth_key = jax.random.fold_in(key, 3)
    field_shape = (SEQUENCE_COUNT, SLOT_LENGTH, heads, HEAD_WIDTH)
    gaussian = jax.random.truncated_normal(first_key, -4.0, 4.0, field_shape, jnp.float32)
    base_noise = gaussian
    row_scale = jnp.exp(jax.random.uniform(third_key, (SEQUENCE_COUNT, SLOT_LENGTH, heads, 1), jnp.float32, math.log(row_low), math.log(row_high)))
    col_scale = jnp.exp(jax.random.uniform(fourth_key, (HEAD_WIDTH,), jnp.float32, math.log(0.3), math.log(3.0)))
    return base_noise * row_scale * col_scale


def draw_key_in(key, part):
    unscaled_block = gained_block(key, 201, KEY_VALUE_HEADS, 0.3, 3.0)
    return unscaled_block.reshape(SEQUENCE_COUNT, SLOT_LENGTH, KEY_VALUE_HEADS * HEAD_WIDTH).astype(jnp.bfloat16)


def draw_query_in(key, part):
    key = jax.random.fold_in(key, 1)
    own_field = gained_block(key, 202, QUERY_HEADS, 0.3, 3.0)
    return own_field.reshape(SEQUENCE_COUNT, SLOT_LENGTH, QUERY_HEADS * HEAD_WIDTH).astype(jnp.bfloat16)


def draw_grad_out(key, part):
    owner_ids = owner_list(key)
    key = jax.random.fold_in(key, 4)
    base_noise = jax.random.truncated_normal(key, -4.0, 4.0, (SEQUENCE_COUNT, SLOT_LENGTH, QUERY_HEADS * HEAD_WIDTH), jnp.float32)
    rise_rate = 2.0
    rise_scale = 1.0 + rise_rate * owner_ids.astype(jnp.float32) / max(SEQUENCE_COUNT // SEQ_DEV - 1, 1)
    return (base_noise * rise_scale[:, None, None]).astype(jnp.bfloat16)


def draw_owners(key, part):
    owner_ids = owner_list(key)
    return owner_ids


def draw_q_gain(key, part):
    key = jax.random.fold_in(key, 6)
    lowest, highest = (0.5, 2.0)
    return jnp.exp(jax.random.uniform(key, (HEAD_WIDTH,), jnp.float32, math.log(lowest), math.log(highest)))


def draw_k_gain(key, part):
    key = jax.random.fold_in(key, 8)
    lowest, highest = (0.5, 2.0)
    return jnp.exp(jax.random.uniform(key, (HEAD_WIDTH,), jnp.float32, math.log(lowest), math.log(highest)))


def plant(entries, own_key, least, high):
    index_at = [jax.random.randint(jax.random.fold_in(own_key, axis), (), 0, length) for axis, length in enumerate(entries.shape)]
    main_axis = entries.shape.index(max(entries.shape))
    next_to = index_at[:main_axis] + [(index_at[main_axis] + 1) % entries.shape[main_axis]] + index_at[main_axis + 1:]
    return entries.at[tuple(index_at)].set(least).at[tuple(next_to)].set(high)


def levels(key, extent, pieces, smallest, top_value):
    level = 1.0
    for position, blocks in pieces:
        heights = jax.random.uniform(jax.random.fold_in(jax.random.fold_in(key, 6), position), (blocks,), jnp.float32, smallest / len(pieces), top_value / len(pieces))
        level = level * jnp.repeat(jnp.exp(heights), extent[position] // blocks).reshape((-1,) + (1,) * (len(extent) - 1 - position))
    return level


def split_up(number_of, total, reach, lean):
    loads = [(1 << 20) // math.isqrt(grade ** lean) + 1 for grade in range(2, number_of + 1)]
    rest, holding = total - reach - (number_of - 1), [1] * (number_of - 1)
    while rest > 0:
        free = [i for i in range(number_of - 1) if holding[i] < reach]
        pool, budget = sum([loads[i] for i in free]), rest
        for i in free:
            extra = min(reach - holding[i], max(1, budget * loads[i] // pool), rest)
            holding[i] = holding[i] + extra
            rest = rest - extra
    return np.array([reach] + holding)


def uneven(stream_key, number_of, total, bound, skew):
    if number_of == 2:
        one = jax.random.randint(stream_key, (), max(1, total - bound), min(bound, total - 1) + 1)
        return jnp.stack([one, total - one])
    sizes = jnp.asarray(split_up(number_of, total, bound, skew), jnp.int32)
    couples = (number_of - 1) // 2
    donor, receiver = sizes[1:1 + 2 * couples:2], sizes[2:2 + 2 * couples:2]
    room = jnp.minimum(donor - 1, bound - receiver)
    passed = jax.random.randint(jax.random.fold_in(stream_key, 1), (couples,), 0, 1 << 20) % (room + 1)
    sizes = sizes.at[1:1 + 2 * couples:2].set(donor - passed).at[2:2 + 2 * couples:2].set(receiver + passed)
    return sizes[jax.random.permutation(jax.random.fold_in(stream_key, 2), number_of)]


def scatter_about(own_key, shape, width, reach, cuts=(), kind=jnp.bfloat16):
    entries = width * jax.random.normal(own_key, shape, jnp.float32)
    if cuts:
        entries = entries * levels(own_key, shape, cuts, -0.22, 0.18)
    return jnp.clip(entries, -reach, reach).astype(kind)


def setup_inputs(seed: int = 0) -> dict:
    key_list = jax.random.split(jax.random.key(seed), 10)
    return {
        "query_in": draw_query_in(jax.random.fold_in(key_list[9], 71), 0),
        "key_in": draw_key_in(jax.random.fold_in(key_list[9], 71), 0),
        "value_input": scatter_about(key_list[2], (SEQUENCE_COUNT, SLOT_LENGTH, KEY_VALUE_HEADS * HEAD_WIDTH), 1.0, 6.0, ((1, 32), (2, 8))),
        "grad_out": draw_grad_out(jax.random.fold_in(key_list[9], 71), 0),
        "q_gain": draw_q_gain(jax.random.fold_in(key_list[9], 71), 0),
        "k_gain": draw_k_gain(jax.random.fold_in(key_list[9], 71), 0),
        "lengths": plant(jax.random.randint(key_list[6], (SEQUENCE_COUNT,), SLOT_LENGTH // 2, SLOT_LENGTH + 1), jax.random.fold_in(key_list[6], 1), SLOT_LENGTH // 2, SLOT_LENGTH).astype(jnp.int32),
        "owners": draw_owners(jax.random.fold_in(key_list[9], 71), 0),
        "doc_ids": jax.vmap(lambda own: jnp.searchsorted(jnp.cumsum(uneven(own, DOCS, SLOT_LENGTH, SLOT_LENGTH // 2, 2)), jnp.arange(SLOT_LENGTH), side="right"))(jax.random.split(key_list[8], SEQUENCE_COUNT)).reshape((SEQUENCE_COUNT, SLOT_LENGTH)).astype(jnp.int32),
    }


EPSILON = 1e-06
NEG_FILL = -1e+30

def apply_rms_norm(values):
    inverse = lax.rsqrt(lax.optimization_barrier(jnp.mean(values * values, axis=-1, keepdims=True)) + EPSILON)
    return (values * inverse, inverse)

def unnormalize(grad_normed, gain_vec, normed, inverse):
    grad_hat = grad_normed * gain_vec
    inner_mean = lax.optimization_barrier(jnp.mean(grad_hat * normed, axis=-1, keepdims=True))
    return inverse * (grad_hat - normed * inner_mean)

def allowed_pairs(doc_row, live_len):
    positions = jnp.arange(doc_row.shape[0], dtype=jnp.int32)
    same_doc = doc_row[:, None] == doc_row[None, :]
    causal = positions[None, :] <= positions[:, None]
    alive_pos = positions < live_len
    return same_doc & causal & alive_pos[:, None] & alive_pos[None, :]

def probabilities(query_head, key_head, allowed):
    score_scale = 1.0 / math.sqrt(query_head.shape[-1])
    scores = jnp.dot(query_head, key_head.T, preferred_element_type=jnp.float32) * score_scale
    scores = jnp.where(allowed, scores, NEG_FILL)
    largest = lax.optimization_barrier(jnp.max(scores, axis=1, keepdims=True))
    weights = jnp.where(allowed, jnp.exp(scores - largest), 0.0)
    row_total = jnp.maximum(lax.optimization_barrier(jnp.sum(weights, axis=1, keepdims=True)), 1.0)
    return weights / row_total

def backward_from(query_head, key_head, value_head, grad_head, weights_norm, weights_low, attention_output):
    score_scale = 1.0 / math.sqrt(query_head.shape[-1])
    grad_probs = jnp.dot(grad_head, value_head.T, preferred_element_type=jnp.float32)
    row_delta = lax.optimization_barrier(jnp.sum(grad_head.astype(jnp.float32) * attention_output, axis=1, keepdims=True))
    grad_scores = (weights_norm * (grad_probs - row_delta)).astype(jnp.bfloat16)
    grad_query = jnp.dot(grad_scores, key_head, preferred_element_type=jnp.float32) * score_scale
    grad_key = jnp.dot(grad_scores.T, query_head, preferred_element_type=jnp.float32) * score_scale
    grad_value = jnp.dot(weights_low.T, grad_head, preferred_element_type=jnp.float32)
    return (grad_query, grad_key, grad_value)

def attend(query_head, key_head, value_head, grad_head, allowed):
    weights_norm = probabilities(query_head, key_head, allowed)
    weights_low = weights_norm.astype(jnp.bfloat16)
    attention_output = jnp.dot(weights_low, value_head, preferred_element_type=jnp.float32)
    grads = backward_from(query_head, key_head, value_head, grad_head, weights_norm, weights_low, attention_output)
    return (attention_output,) + grads

def sequence_pass(query_row, key_row_view, value_row_view, grad_row, doc_row, live_len, q_gain, k_gain):
    slot_width = query_row.shape[0]
    group_width = QUERY_HEADS // KEY_VALUE_HEADS
    q_hat, q_inv = apply_rms_norm(query_row.astype(jnp.float32).reshape(slot_width, QUERY_HEADS, HEAD_WIDTH))
    key_unit_rows, key_inverse_norm = apply_rms_norm(key_row_view.astype(jnp.float32).reshape(slot_width, KEY_VALUE_HEADS, HEAD_WIDTH))
    q_normed = (q_hat * q_gain).astype(jnp.bfloat16)
    k_normed = (key_unit_rows * k_gain).astype(jnp.bfloat16)
    value_head_rows = value_row_view.reshape(slot_width, KEY_VALUE_HEADS, HEAD_WIDTH)
    grad_heads = grad_row.reshape(slot_width, QUERY_HEADS, HEAD_WIDTH)
    allowed = allowed_pairs(doc_row, live_len)

    def one_head(head_idx):
        kv_idx = head_idx // group_width
        return attend(q_normed[:, head_idx], k_normed[:, kv_idx], value_head_rows[:, kv_idx], grad_heads[:, head_idx], allowed)
    attention_output, grad_qn, normed_key_gradient, value_head_gradient = lax.map(one_head, jnp.arange(QUERY_HEADS, dtype=jnp.int32))
    attention_output = jnp.transpose(attention_output, (1, 0, 2))
    grad_qn = jnp.transpose(grad_qn, (1, 0, 2))
    normed_key_gradient = jnp.transpose(lax.optimization_barrier(jnp.sum(normed_key_gradient.reshape(KEY_VALUE_HEADS, group_width, slot_width, HEAD_WIDTH), axis=1)), (1, 0, 2))
    value_head_gradient = jnp.transpose(lax.optimization_barrier(jnp.sum(value_head_gradient.reshape(KEY_VALUE_HEADS, group_width, slot_width, HEAD_WIDTH), axis=1)), (1, 0, 2))
    query_gradient_packed = unnormalize(grad_qn, q_gain, q_hat, q_inv).astype(jnp.bfloat16)
    key_gradient_packed = unnormalize(normed_key_gradient, k_gain, key_unit_rows, key_inverse_norm).astype(jnp.bfloat16)
    query_correction = lax.optimization_barrier(jnp.sum(grad_qn * q_hat, axis=(0, 1)))
    key_correction = lax.optimization_barrier(jnp.sum(normed_key_gradient * key_unit_rows, axis=(0, 1)))
    return (attention_output.astype(jnp.bfloat16).reshape(slot_width, QUERY_HEADS * HEAD_WIDTH), query_gradient_packed.reshape(slot_width, QUERY_HEADS * HEAD_WIDTH), key_gradient_packed.reshape(slot_width, KEY_VALUE_HEADS * HEAD_WIDTH), value_head_gradient.astype(jnp.bfloat16).reshape(slot_width, KEY_VALUE_HEADS * HEAD_WIDTH), query_correction, key_correction)

def reference(query_in, key_in, value_input, grad_out, q_gain, k_gain, lengths, owners, doc_ids):
    packed_order = jnp.argsort(owners, stable=True).astype(jnp.int32)

    def one_sequence(seq_idx):
        return sequence_pass(query_in[seq_idx], key_in[seq_idx], value_input[seq_idx], grad_out[seq_idx], doc_ids[seq_idx], lengths[seq_idx], q_gain, k_gain)
    attention, query_gradient_packed, key_gradient_packed, value_grad, q_terms, key_corrections = lax.map(one_sequence, packed_order)
    q_gain_grad = lax.optimization_barrier(jnp.sum(q_terms, axis=0)) / math.sqrt(SEQUENCE_COUNT * SLOT_LENGTH * QUERY_HEADS)
    key_gain_gradient = lax.optimization_barrier(jnp.sum(key_corrections, axis=0)) / math.sqrt(SEQUENCE_COUNT * SLOT_LENGTH * KEY_VALUE_HEADS)
    return (attention, query_gradient_packed, key_gradient_packed, value_grad, q_gain_grad, key_gain_gradient)
```

```python
import functools
import math

import jax
import jax.numpy as jnp
from jax import lax
from jax.experimental import pallas as pl
from jax.experimental.pallas import tpu as pltpu
from jax.sharding import PartitionSpec as P

WIDTH = 128
SLOT = 1024
TILE = 256
REACH = 512
EPSILON = 1e-06
NEG_FILL = -1e30
SCALE = 1.0 / math.sqrt(WIDTH)
BF = jnp.bfloat16
F32 = jnp.float32


def rms(rows):
    values = rows.astype(F32)
    inverse = lax.rsqrt(jnp.mean(values * values, axis=-1, keepdims=True) + EPSILON)
    return values * inverse, inverse


def unnormalize(grad_normed, gain, normed, inverse):
    grad_hat = grad_normed * gain
    inner = jnp.mean(grad_hat * normed, axis=-1, keepdims=True)
    return inverse * (grad_hat - normed * inner)


def pack_first(owners, key, value, query, grad, out):
    for s in range(key.shape[0]):
        o = owners[s]
        out[o, 0] = key[s]
        out[o, 1] = value[s]
        out[o, 2] = query[s]
        out[o, 3] = grad[s]


def pack_rest(owners, query, grad, *outs):
    for s in range(query.shape[0]):
        o = owners[s]
        for h, out in enumerate(outs):
            cols = pl.ds(h * WIDTH, WIDTH)
            out[o, 0] = query[s, :, cols]
            out[o, 1] = grad[s, :, cols]


def dot(a, b):
    return jnp.dot(a, b, preferred_element_type=F32)


def dot_t(a, b):
    return lax.dot_general(a, b, (((1,), (1,)), ((), ())), preferred_element_type=F32)


def attend(head, last, *refs):
    refs = list(refs)
    live, doc, q_gain, k_gain, kv = refs[:5]
    del refs[:5]
    if head == 0:
        own, q_slot, g_slot = kv, 2, 3
    else:
        own, q_slot, g_slot = refs.pop(0), 0, 1
        dk_in, dv_in, qs_in = refs[:3]
        del refs[:3]
    send = refs.pop(0)
    if last:
        kv_send, sums = refs[:2]
    else:
        dk, dv, qs = refs[:3]
    del refs[: 2 if last else 3]
    if last:
        kn, knt, vt, dk, dv = refs
    else:
        kn, knt, vt = refs

    def rows(ref, slot, at, size):
        return ref[at // 32 : (at + size) // 32, slot].reshape(size, WIDTH)

    doc_row = doc[...]
    start = jnp.zeros_like(doc_row)
    for d in range(8):
        count = jnp.sum((doc_row == d).astype(jnp.int32), axis=1, keepdims=True)
        start = start + jnp.where(doc_row > d, count, 0)
    length = live[0]
    if head == 0:
        dk[...] = jnp.zeros_like(dk)
        dv[...] = jnp.zeros_like(dv)
        q_sum = jnp.zeros((1, WIDTH), F32)
    else:
        dk[...] = dk_in[...]
        dv[...] = dv_in[...]
        q_sum = qs_in[...]
    for at in range(0, SLOT, TILE):
        part = pl.ds(at, TILE)
        k_hat, _ = rms(rows(kv, 0, at, TILE))
        normed = k_hat * k_gain[...]
        kn[part] = normed.astype(BF)
        knt[:, part] = normed.T.astype(BF)
        vt[:, part] = rows(kv, 1, at, TILE).astype(F32).T.astype(BF)
    u_rel = lax.broadcasted_iota(jnp.int32, (TILE, TILE), 0)
    t_rel = lax.broadcasted_iota(jnp.int32, (1, TILE), 1)
    for t0 in range(0, SLOT, TILE):
        u_list = [u for u in range(0, t0 + 1, TILE) if t0 - (u + TILE - 1) < REACH]
        q_hat, q_inv = rms(rows(own, q_slot, t0, TILE))
        q_n = (q_hat * q_gain[...]).astype(BF)
        g = rows(own, g_slot, t0, TILE)
        g_t = g.astype(F32).T
        g_tb = g_t.astype(BF)
        first = start[:, t0 : t0 + TILE]
        scores = []
        for u0 in u_list:
            s = dot_t(kn[pl.ds(u0, TILE)], q_n) * (SCALE * math.log2(math.e))
            allowed = u_rel >= first - u0
            if u0 == t0:
                allowed = allowed & (u_rel <= t_rel)
            scores.append(jnp.where(allowed, s, NEG_FILL))
        largest = functools.reduce(
            jnp.maximum, [jnp.max(s, axis=0, keepdims=True) for s in scores]
        )
        weights = [jnp.exp2(s - largest) for s in scores]
        total = sum(jnp.sum(w, axis=0, keepdims=True) for w in weights)
        factor = jnp.where(t_rel + t0 < length, 1.0 / jnp.maximum(total, 1.0), 0.0)
        probs = [w * factor for w in weights]
        low = [p.astype(BF) for p in probs]
        o_t = sum(dot(vt[:, pl.ds(u0, TILE)], p) for u0, p in zip(u_list, low))
        delta = jnp.sum(g_t * o_t, axis=0, keepdims=True)
        dq_t = 0.0
        for u0, p, pb in zip(u_list, probs, low):
            part = pl.ds(u0, TILE)
            dv[part] += dot(pb, g)
            dp = dot(rows(kv, 1, u0, TILE), g_tb)
            ds = (p * (dp - delta)).astype(BF)
            dk[part] += dot(ds, q_n)
            dq_t += dot(knt[:, part], ds)
        dq = dq_t.T * SCALE
        q_sum += jnp.sum(dq * q_hat, axis=0, keepdims=True)
        dq = unnormalize(dq, q_gain[...], q_hat, q_inv).astype(BF)
        o = o_t.T.astype(BF)
        for n in range(TILE // WIDTH):
            block = t0 // WIDTH + n
            send[block, 0] = o[n * WIDTH : (n + 1) * WIDTH]
            send[block, 1] = dq[n * WIDTH : (n + 1) * WIDTH]
    if not last:
        qs[...] = q_sum
        return
    k_sum = jnp.zeros((1, WIDTH), F32)
    for at in range(0, SLOT, WIDTH):
        part = pl.ds(at, WIDTH)
        k_hat, k_inv = rms(rows(kv, 0, at, WIDTH))
        gk = dk[part] * SCALE
        k_sum += jnp.sum(gk * k_hat, axis=0, keepdims=True)
        kv_send[at // WIDTH, 0] = unnormalize(gk, k_gain[...], k_hat, k_inv).astype(BF)
        kv_send[at // WIDTH, 1] = dv[part].astype(BF)
    sums[0:1] = q_sum
    sums[1:2] = k_sum


def place(*refs):
    heads = len(refs) - 5
    received, kv, outs = refs[:heads], refs[heads], refs[heads + 1 :]
    for src in range(kv.shape[0]):
        for h, ref in enumerate(received):
            cols = pl.ds((src * heads + h) * WIDTH, WIDTH)
            outs[0][0, :, cols] = ref[src, 0]
            outs[1][0, :, cols] = ref[src, 1]
        cols = pl.ds(src * WIDTH, WIDTH)
        outs[2][0, :, cols] = kv[src, 0]
        outs[3][0, :, cols] = kv[src, 1]


def params():
    return pltpu.CompilerParams(vmem_limit_bytes=32 * 1024 * 1024)


def shape(dims, dtype=BF):
    return jax.ShapeDtypeStruct(dims, dtype)


def attend_head(head, last, live, doc, q_gain, k_gain, kv, own, carry):
    args = [live, doc, q_gain, k_gain, kv]
    if head > 0:
        args += [own, *carry]
    blocks = SLOT // WIDTH
    outs = [shape((blocks, 2, WIDTH, WIDTH))]
    if last:
        outs += [shape((blocks, 2, WIDTH, WIDTH)), shape((2, WIDTH), F32)]
    else:
        outs += [shape((SLOT, WIDTH), F32), shape((SLOT, WIDTH), F32), shape((1, WIDTH), F32)]
    scratch = [
        pltpu.VMEM((SLOT, WIDTH), BF),
        pltpu.VMEM((WIDTH, SLOT), BF),
        pltpu.VMEM((WIDTH, SLOT), BF),
    ]
    if last:
        scratch += [pltpu.VMEM((SLOT, WIDTH), F32), pltpu.VMEM((SLOT, WIDTH), F32)]
    return pl.pallas_call(
        functools.partial(attend, head, last),
        out_shape=outs,
        in_specs=[pl.BlockSpec(memory_space=pltpu.SMEM)]
        + [pl.BlockSpec(memory_space=pltpu.VMEM)] * (len(args) - 1),
        out_specs=[pl.BlockSpec(memory_space=pltpu.VMEM)] * len(outs),
        scratch_shapes=scratch,
        compiler_params=params(),
        cost_estimate=pl.CostEstimate(
            flops=12 * 9 * TILE * TILE * WIDTH, bytes_accessed=4 << 20, transcendentals=9 * TILE * TILE
        ),
        name="attend",
    )(*args)


def per_device(query, key, value, grad, q_gain, k_gain, lengths, owners, doc_ids):
    seqs, per_src, features = query.shape
    heads = features // WIDTH
    head_devs = lax.axis_size("head")
    vmem = pl.BlockSpec(memory_space=pltpu.VMEM)
    smem = pl.BlockSpec(memory_space=pltpu.SMEM)
    one = pl.BlockSpec((seqs, per_src, WIDTH), lambda n: (0, 0, 0))
    first = pl.pallas_call(
        pack_first,
        grid=(1,),
        out_shape=shape((seqs, 4, per_src, WIDTH)),
        in_specs=[smem, one, one, one, one],
        out_specs=pl.BlockSpec((seqs, 4, per_src, WIDTH), lambda n: (0, 0, 0, 0)),
        compiler_params=params(),
        name="pack_first",
    )(owners, key, value, query, grad)
    rest = pl.pallas_call(
        pack_rest,
        out_shape=[shape((seqs, 2, per_src, WIDTH))] * (heads - 1),
        in_specs=[smem, vmem, vmem],
        out_specs=[vmem] * (heads - 1),
        compiler_params=params(),
        name="pack_rest",
    )(owners, query[:, :, WIDTH:], grad[:, :, WIDTH:])

    mine = jnp.argmax(owners == lax.axis_index("dp")).astype(jnp.int32)
    live = lax.dynamic_slice_in_dim(lengths, mine, 1)
    doc = lax.dynamic_slice_in_dim(doc_ids, mine, 1, axis=0)
    q_gain = q_gain.reshape(1, WIDTH)
    k_gain = k_gain.reshape(1, WIDTH)

    kv = lax.all_to_all(first, "dp", 0, 0, tiled=True)
    own = [None] + [lax.all_to_all(r, "dp", 0, 0, tiled=True) for r in rest]
    received, carry = [], None
    for h in range(heads):
        last = h == heads - 1
        out, *carry = attend_head(h, last, live, doc, q_gain, k_gain, kv, own[h], carry)
        received.append(lax.all_to_all(out, "head", 0, 0, tiled=True))
    kv_send, sums = carry
    received.append(lax.all_to_all(kv_send, "head", 0, 0, tiled=True))
    sums = lax.psum(sums, ("dp", "head"))
    wide, narrow = shape((1, WIDTH, heads * head_devs * WIDTH)), shape((1, WIDTH, head_devs * WIDTH))
    outs = pl.pallas_call(
        place,
        out_shape=[wide, wide, narrow, narrow],
        in_specs=[vmem] * len(received),
        out_specs=[vmem] * 4,
        compiler_params=params(),
        name="place",
    )(*received)
    tokens = seqs * SLOT
    return (
        *outs,
        sums[0] / math.sqrt(tokens * heads * head_devs),
        sums[1] / math.sqrt(tokens * head_devs),
    )


def solution(mesh):
    spread = P(None, "dp", "head")
    packed = P("dp", "head", None)
    return jax.shard_map(
        per_device,
        mesh=mesh,
        in_specs=(spread,) * 4 + (P(),) * 5,
        out_specs=(packed,) * 4 + (P(),) * 2,
        check_vma=False,
    )
```

```python
import functools
import math

import jax
import jax.numpy as jnp
from jax import lax
from jax.experimental import pallas as pl
from jax.experimental.pallas import tpu as pltpu
from jax.sharding import PartitionSpec as P

WIDTH = 128
SLOT = 1024
TILE = 256
REACH = 512
CHUNKS = (3, 1)
EPSILON = 1e-06
NEG_FILL = -1e30
SCALE = 1.0 / math.sqrt(WIDTH)
BF = jnp.bfloat16
F32 = jnp.float32


def rms(rows):
    values = rows.astype(F32)
    inverse = lax.rsqrt(jnp.mean(values * values, axis=-1, keepdims=True) + EPSILON)
    return values * inverse, inverse


def unnormalize(grad_normed, gain, normed, inverse):
    grad_hat = grad_normed * gain
    inner = jnp.mean(grad_hat * normed, axis=-1, keepdims=True)
    return inverse * (grad_hat - normed * inner)


def dot(a, b):
    return jnp.dot(a, b, preferred_element_type=F32)


def dot_t(a, b):
    return lax.dot_general(a, b, (((1,), (1,)), ((), ())), preferred_element_type=F32)


def identity(size):
    row = lax.broadcasted_iota(jnp.int32, (size, size), 0)
    col = lax.broadcasted_iota(jnp.int32, (size, size), 1)
    return (row == col).astype(F32).astype(BF)


def start_all(copies):
    for copy in copies:
        copy.start()


def wait_all(copies):
    for copy in copies:
        copy.wait()


def pack(pieces, owners, *refs):
    *arrays, out, stage, in_sems, out_sems = refs
    seqs = stage.shape[0]
    groups = in_sems.shape[0]
    span = seqs // groups
    loads = [
        [
            pltpu.make_async_copy(
                ref.at[pl.ds(g * span, span), :, pl.ds(at, size)],
                stage.at[pl.ds(g * span, span), :, pl.ds(to, size)],
                in_sems.at[g, n],
            )
            for n, (ref, (at, to, size)) in enumerate(zip(arrays, pieces))
        ]
        for g in range(groups)
    ]
    for group in loads:
        start_all(group)
    stores = []
    for g, group in enumerate(loads):
        wait_all(group)
        for s in range(g * span, (g + 1) * span):
            stores.append(pltpu.make_async_copy(stage.at[s], out.at[owners[s]], out_sems.at[s]))
            stores[-1].start()
    wait_all(stores)


def my_place():
    head = lax.axis_index("head")
    return head // 2, lax.rem(head, 2)


def attend(heads, first, last, *refs):
    refs = list(refs)
    owners, lengths, docs, q_gain, k_gain, kv_hbm = refs[:6]
    del refs[:6]
    own_hbm = kv_hbm if first else refs.pop(0)
    if not first:
        carry_in = refs[:6]
        del refs[:6]
    outs = refs[:8]
    del refs[:8]
    if last:
        sums = refs.pop(0)
    else:
        carry_out = refs[:6]
        del refs[:6]
    kv, own, send, kn, knt, vt, dk, dv, q_acc, in_sems, carry_sems, out_sem = refs
    kept = (kn, knt, vt, dk, dv, q_acc)

    def column(n):
        return pl.ds(n * WIDTH, WIDTH)

    base = kv_hbm.shape[2] // WIDTH - 2
    kv_in = [
        pltpu.make_async_copy(kv_hbm.at[:, :, column(base + n)], kv.at[n], in_sems.at[n])
        for n in range(2)
    ]
    own_in = [
        pltpu.make_async_copy(own_hbm.at[:, :, column(n)], own.at[n], in_sems.at[n + 2])
        for n in (m for h in range(heads) for m in (h, heads + h))
    ]
    start_all(kv_in + own_in)
    if not first:
        carry = [
            pltpu.make_async_copy(a, b, carry_sems.at[n])
            for n, (a, b) in enumerate(zip(carry_in, kept))
        ]
        start_all(carry)

    eye = identity(WIDTH)
    eye_tile = identity(TILE)

    def rows(ref, slot, at, size):
        return ref[slot, at // 32 : (at + size) // 32].reshape(size, WIDTH)

    mine = jnp.int32(0)
    for s in range(owners.shape[0]):
        mine = jnp.where(owners[s] == lax.axis_index("dp"), s, mine)
    length = lengths[mine]
    doc_row = docs[pl.ds(mine, 1)]
    start = jnp.zeros_like(doc_row)
    for d in range(8):
        count = jnp.sum((doc_row == d).astype(jnp.int32), axis=1, keepdims=True)
        start = start + jnp.where(doc_row > d, count, 0)
    gain = jnp.broadcast_to(q_gain[...], (TILE, WIDTH)).T
    y, c = my_place()
    if first:
        dk[...] = jnp.zeros_like(dk)
        dv[...] = jnp.zeros_like(dv)
        q_acc[...] = jnp.zeros_like(q_acc)
        wait_all(kv_in)
        for at in range(0, SLOT, TILE):
            part = pl.ds(at, TILE)
            normed = (rms(rows(kv, 0, at, TILE))[0] * k_gain[...]).astype(BF)
            kn[part] = normed
            knt[:, part] = dot_t(eye, normed).astype(BF)
            vt[:, part] = dot_t(eye, rows(kv, 1, at, TILE)).astype(BF)
    else:
        wait_all(kv_in + carry)
    wait_all(own_in)
    u_rel = lax.broadcasted_iota(jnp.int32, (TILE, TILE), 0)
    t_rel = lax.broadcasted_iota(jnp.int32, (1, TILE), 1)

    def copies_out(n):
        cols = pl.ds(pl.multiple_of(n * WIDTH, WIDTH), WIDTH)
        return [
            pltpu.make_async_copy(
                send.at[lax.rem(y + r // 2, 4), c ^ (r % 2), :, cols], out.at[:, cols], out_sem.at[r]
            )
            for r, out in enumerate(outs)
        ]

    def one_head(h):
        for t0 in range(0, SLOT, TILE):
            u_list = [u for u in range(0, t0 + 1, TILE) if t0 - (u + TILE - 1) < REACH]
            q_t = dot_t(eye, rows(own, h, t0, TILE))
            g_t = dot_t(eye, rows(own, heads + h, t0, TILE))
            g_b = g_t.astype(BF)
            q_inv = lax.rsqrt(jnp.mean(q_t * q_t, axis=0, keepdims=True) + EPSILON)
            q_hat = q_t * q_inv
            q_n = (q_hat * gain).astype(BF)
            starts = start[:, t0 : t0 + TILE]
            scores = [dot(kn[pl.ds(u0, TILE)], q_n) for u0 in u_list]
            grads = [dot(rows(kv, 1, u0, TILE), g_b) for u0 in u_list]
            masked = []
            for u0, s in zip(u_list, scores):
                allowed = u_rel >= starts - u0
                if u0 == t0:
                    allowed = allowed & (u_rel <= t_rel)
                masked.append(jnp.where(allowed, s * (SCALE * math.log2(math.e)), NEG_FILL))
            largest = functools.reduce(
                jnp.maximum, [jnp.max(s, axis=0, keepdims=True) for s in masked]
            )
            weights = [jnp.exp2(s - largest) for s in masked]
            total = sum(jnp.sum(w, axis=0, keepdims=True) for w in weights)
            factor = jnp.where(t_rel + t0 < length, 1.0 / jnp.maximum(total, 1.0), 0.0)
            probs = [w * factor for w in weights]
            low = [p.astype(BF) for p in probs]
            o_t = sum(dot(vt[:, pl.ds(u0, TILE)], p) for u0, p in zip(u_list, low))
            delta = jnp.sum(g_t * o_t, axis=0, keepdims=True)
            dq_t = 0.0
            for u0, p, pb, dp in zip(u_list, probs, low, grads):
                part = pl.ds(u0, TILE)
                dv[part] += dot_t(pb, g_b)
                ds = (p * (dp - delta)).astype(BF)
                dk[part] += dot_t(ds, q_n)
                dq_t += dot(knt[:, part], ds)
            dq_t = dq_t * SCALE
            q_acc[...] += dq_t * q_hat
            grad_hat = dq_t * gain
            inner = jnp.mean(grad_hat * q_hat, axis=0, keepdims=True)
            dq = (q_inv * (grad_hat - q_hat * inner)).astype(BF)
            o = dot_t(eye_tile, o_t.astype(BF)).astype(BF)
            dq = dot_t(eye_tile, dq).astype(BF)
            for n in range(TILE // WIDTH):
                for to, block in ((h, o), (heads + h, dq)):
                    cols = pl.ds(pl.multiple_of(to * WIDTH, WIDTH), WIDTH)
                    send[t0 // TILE, n, :, cols] = block[n * WIDTH : (n + 1) * WIDTH]
        start_all(copies_out(h) + copies_out(heads + h))

    def finish():
        k_sum = jnp.zeros((1, WIDTH), F32)
        for at in range(0, SLOT, WIDTH):
            part = pl.ds(at, WIDTH)
            k_hat, k_inv = rms(rows(kv, 0, at, WIDTH))
            gk = dk[part] * SCALE
            k_sum += jnp.sum(gk * k_hat, axis=0, keepdims=True)
            block = at // TILE, at // WIDTH % 2, slice(None)
            grad_k = unnormalize(gk, k_gain[...], k_hat, k_inv).astype(BF)
            send[(*block, column(2 * heads))] = grad_k
            send[(*block, column(2 * heads + 1))] = dv[part].astype(BF)
        start_all(copies_out(2 * heads) + copies_out(2 * heads + 1))
        q_sum = jnp.sum(q_acc[...], axis=1, keepdims=True)
        sums[0:1] = jnp.broadcast_to(q_sum, (WIDTH, WIDTH)).T[0:1]
        sums[1:2] = k_sum

    if heads == 1:
        one_head(0)
    else:
        pl.loop(0, heads)(one_head)
    if last:
        finish()
    else:
        carry = [
            pltpu.make_async_copy(b, a, carry_sems.at[n])
            for n, (a, b) in enumerate(zip(carry_out, kept))
        ]
        start_all(carry)
        wait_all(carry)
    for r, out in enumerate(outs):
        pltpu.make_async_copy(out, out, out_sem.at[r]).wait()


def place(at, *refs):
    refs = list(refs)
    stage, in_sems, out_sems = refs[-3:]
    received, outs = refs[:8], refs[-7:-3]
    y, c = my_place()
    columns = outs[0].shape[2] // (8 * WIDTH) * WIDTH
    count = 2 if at == 0 else 4
    per = received[0].shape[1] // count
    loads = [
        pltpu.make_async_copy(ref, stage.at[r], in_sems.at[r]) for r, ref in enumerate(received)
    ]
    start_all(loads)
    stores = []
    for r, load in enumerate(loads):
        load.wait()
        src = lax.rem(y + 4 - r // 2, 4) * 2 + (c ^ (r % 2))
        for n in range(count):
            start = src * columns + at if n < 2 else src * WIDTH
            stores.append(
                pltpu.make_async_copy(
                    stage.at[r, :, pl.ds(n * per, per)],
                    outs[n].at[0, :, pl.ds(pl.multiple_of(start, WIDTH), per)],
                    out_sems.at[r, n],
                )
            )
            stores[-1].start()
    wait_all(stores)


HBM = pl.BlockSpec(memory_space=pltpu.HBM)
VMEM = pl.BlockSpec(memory_space=pltpu.VMEM)
SMEM = pl.BlockSpec(memory_space=pltpu.SMEM)


def call(kernel, args, in_specs, outs, out_specs, scratch=(), name=None, flops=0, aliases=None):
    moved = sum(math.prod(a.shape) * a.dtype.itemsize for a in (*args, *outs))
    return pl.pallas_call(
        kernel,
        out_shape=outs,
        in_specs=in_specs,
        out_specs=out_specs,
        scratch_shapes=scratch,
        input_output_aliases=aliases or {},
        compiler_params=pltpu.CompilerParams(vmem_limit_bytes=60 * 1024 * 1024),
        cost_estimate=pl.CostEstimate(flops=flops, bytes_accessed=moved, transcendentals=0),
        name=name,
    )(*args)


def shape(dims, dtype=BF):
    return jax.ShapeDtypeStruct(dims, dtype)


def attend_chunk(heads, first, last, owners, lengths, docs, q_gain, k_gain, kv, own, carry):
    args = [owners, lengths, docs, q_gain, k_gain, kv]
    if not first:
        args += [own, *carry]
    width = (2 * heads + (2 if last else 0)) * WIDTH
    outs = [shape((WIDTH, width))] * 8
    kept = [
        ((SLOT, WIDTH), BF),
        ((WIDTH, SLOT), BF),
        ((WIDTH, SLOT), BF),
        ((SLOT, WIDTH), F32),
        ((SLOT, WIDTH), F32),
        ((WIDTH, TILE), F32),
    ]
    per_src = kv.shape[1]
    scratch = [
        pltpu.VMEM((2, SLOT // per_src, per_src, WIDTH), BF),
        pltpu.VMEM((2 * heads, SLOT // per_src, per_src, WIDTH), BF),
        pltpu.VMEM((4, 2, WIDTH, width), BF),
        *(pltpu.VMEM(*a) for a in kept),
        pltpu.SemaphoreType.DMA((2 + 2 * heads,)),
        pltpu.SemaphoreType.DMA((len(kept),)),
        pltpu.SemaphoreType.DMA((8,)),
    ]
    outs += [shape((2, WIDTH), F32)] if last else [shape(*a) for a in kept]
    result = call(
        functools.partial(attend, heads, first, last),
        args,
        [SMEM, SMEM, VMEM, VMEM, VMEM] + [HBM] * (len(args) - 5),
        outs,
        [HBM] * 8 + ([VMEM] if last else [HBM] * len(kept)),
        scratch,
        "attend",
        heads * 12 * 9 * TILE * TILE * WIDTH,
    )
    return result[:8], result[8:]


def across(r):
    return [(i, ((i // 2 + r // 2) % 4) * 2 + ((i % 2) ^ (r % 2))) for i in range(8)]


def packed_chunk(owners, arrays, pieces, name):
    seqs, per_src, _ = arrays[0].shape
    width = sum(p[2] for p in pieces)
    return call(
        functools.partial(pack, pieces),
        [owners, *arrays],
        [SMEM] + [HBM] * len(arrays),
        [shape((seqs, per_src, width))],
        [HBM],
        [
            pltpu.VMEM((seqs, per_src, width), BF),
            pltpu.SemaphoreType.DMA((4, len(pieces))),
            pltpu.SemaphoreType.DMA((seqs,)),
        ],
        name,
    )[0]


def total(sums, axis):
    spread = jnp.broadcast_to(sums, (lax.axis_size(axis), *sums.shape))
    return jnp.sum(lax.all_to_all(spread, axis, 0, 0, tiled=True), axis=0)


def per_device(query, key, value, grad, q_gain, k_gain, lengths, owners, doc_ids):
    seqs, _, features = query.shape
    heads = features // WIDTH
    head_devs = lax.axis_size("head")
    cut, rest = CHUNKS[0] * WIDTH, CHUNKS[1] * WIDTH
    front = packed_chunk(
        owners,
        [query, grad, key, value],
        [(0, 0, cut), (0, cut, cut), (0, 2 * cut, WIDTH), (0, 2 * cut + WIDTH, WIDTH)],
        "pack_front",
    )
    back = packed_chunk(owners, [query, grad], [(cut, 0, rest), (cut, rest, rest)], "pack_back")
    front = lax.all_to_all(front, "dp", 0, 0, tiled=True)
    front, back = lax.optimization_barrier((front, back))
    back = lax.all_to_all(back, "dp", 0, 0, tiled=True)

    small = (owners, lengths, doc_ids, q_gain.reshape(1, WIDTH), k_gain.reshape(1, WIDTH))
    out, carry = attend_chunk(CHUNKS[0], True, False, *small, front, None, None)
    early = [out[0]] + [lax.ppermute(out[r], "head", across(r)) for r in range(1, 8)]
    out, (sums,) = attend_chunk(CHUNKS[1], False, True, *small, front, back, carry)
    late = [out[0]] + [lax.ppermute(out[r], "head", across(r)) for r in range(1, 8)]
    sums, late = lax.optimization_barrier((total(sums, "dp"), late))
    sums = total(sums, "head")
    wide, narrow = shape((1, WIDTH, heads * head_devs * WIDTH)), shape((1, WIDTH, head_devs * WIDTH))
    outs = None
    for at, got in ((0, early), (cut, late)):
        outs = call(
            functools.partial(place, at),
            [*got, *(outs or [])],
            [HBM] * (8 + len(outs or [])),
            [wide, wide, narrow, narrow],
            [HBM] * 4,
            [
                pltpu.VMEM((8, *got[0].shape), BF),
                pltpu.SemaphoreType.DMA((8,)),
                pltpu.SemaphoreType.DMA((8, 4)),
            ],
            "place",
            aliases={8 + n: n for n in range(4)} if outs else None,
        )
    tokens = seqs * SLOT
    return (
        *outs,
        sums[0] / math.sqrt(tokens * heads * head_devs),
        sums[1] / math.sqrt(tokens * head_devs),
    )


def solution(mesh):
    spread = P(None, "dp", "head")
    packed = P("dp", "head", None)
    return jax.shard_map(
        per_device,
        mesh=mesh,
        in_specs=(spread,) * 4 + (P(),) * 5,
        out_specs=(packed,) * 4 + (P(),) * 2,
        check_vma=False,
    )
```

```python
import functools
import math

import jax
import jax.numpy as jnp
from jax import lax
from jax.experimental import pallas as pl
from jax.experimental.pallas import tpu as pltpu
from jax.sharding import Mesh, PartitionSpec as P

WIDTH = 128
SLOT = 1024
TILE = 256
REACH = 512
CHUNKS = (2, 2)
SUM_ROWS = 16
DP = ("z", "x")
GROUPS = ((0, 256, 512, 768),)
EPSILON = 1e-06
NEG_FILL = -1e30
SCALE = 1.0 / math.sqrt(WIDTH)
BF = jnp.bfloat16
F32 = jnp.float32


def rms(rows):
    values = rows.astype(F32)
    inverse = lax.rsqrt(jnp.mean(values * values, axis=-1, keepdims=True) + EPSILON)
    return values * inverse, inverse


def unnormalize(grad_normed, gain, normed, inverse):
    grad_hat = grad_normed * gain
    inner = jnp.mean(grad_hat * normed, axis=-1, keepdims=True)
    return inverse * (grad_hat - normed * inner)


def dot(a, b):
    return jnp.dot(a, b, preferred_element_type=F32)


def dot_t(a, b):
    return lax.dot_general(a, b, (((1,), (1,)), ((), ())), preferred_element_type=F32)


def identity(size):
    row = lax.broadcasted_iota(jnp.int32, (size, size), 0)
    col = lax.broadcasted_iota(jnp.int32, (size, size), 1)
    return (row == col).astype(F32).astype(BF)


def start_all(copies):
    for copy in copies:
        copy.start()


def wait_all(copies):
    for copy in copies:
        copy.wait()


def pack(pieces, owners, *refs):
    arrays, refs = refs[: len(pieces)], refs[len(pieces) :]
    *outs, stage, holder, in_sems, out_sems = refs
    seqs = stage.shape[0]
    groups = in_sems.shape[0]
    span = seqs // groups
    loads = [
        [
            pltpu.make_async_copy(
                ref.at[pl.ds(g * span, span), :, pl.ds(at, size)],
                stage.at[pl.ds(g * span, span), :, pl.ds(to, size)],
                in_sems.at[g, n],
            )
            for n, (ref, (at, to, size)) in enumerate(zip(arrays, pieces))
        ]
        for g in range(groups)
    ]
    for group in loads:
        start_all(group)
    stores = []
    if len(outs) == 1:
        for g, group in enumerate(loads):
            wait_all(group)
            for s in range(g * span, (g + 1) * span):
                copy = pltpu.make_async_copy(stage.at[s], outs[0].at[owners[s]], out_sems.at[s])
                copy.start()
                stores.append(copy)
    else:
        for s in range(seqs):
            holder[owners[s]] = s
        for group in loads:
            wait_all(group)
        for k, out in enumerate(outs):
            x = lax.rem(lax.axis_index("x") + k, len(outs))
            for z in range(out.shape[0]):
                s = holder[z * len(outs) + x]
                copy = pltpu.make_async_copy(stage.at[s], out.at[z], out_sems.at[k * out.shape[0] + z])
                copy.start()
                stores.append(copy)
    wait_all(stores)


def regroup(*refs):
    *arrays, out, stage, in_sems, out_sem = refs
    count = len(arrays)
    loads = []
    for k, ref in enumerate(arrays):
        src = lax.rem(lax.axis_index("x") + count - k, count)
        loads.append(pltpu.make_async_copy(ref, stage.at[:, src], in_sems.at[k]))
    start_all(loads)
    wait_all(loads)
    store = pltpu.make_async_copy(stage, out, out_sem.at[0])
    store.start()
    store.wait()


def my_place():
    head = lax.axis_index("head")
    return head // 2, lax.rem(head, 2)


def attend(heads, first, last, *refs):
    refs = list(refs)
    owners, lengths, docs, q_gain, k_gain, kv_hbm = refs[:6]
    del refs[:6]
    own_hbm = kv_hbm if first else refs.pop(0)
    if not first:
        carry_in = refs[:6]
        del refs[:6]
    outs = refs[:8]
    del refs[:8]
    if last:
        sums = refs.pop(0)
    else:
        carry_out = refs[:6]
        del refs[:6]
    kv, own, send, kn, knt, vt, dk, dv, q_acc, in_sems, carry_sems, out_sem = refs
    kept = (kn, knt, vt, dk, dv, q_acc)

    def column(n):
        return pl.ds(n * WIDTH, WIDTH)

    base = kv_hbm.shape[2] // WIDTH - 2
    kv_in = [
        pltpu.make_async_copy(kv_hbm.at[:, :, column(base + n)], kv.at[n], in_sems.at[n])
        for n in range(2)
    ]
    own_in = [
        pltpu.make_async_copy(own_hbm.at[:, :, column(n)], own.at[n], in_sems.at[n + 2])
        for n in (m for h in range(heads) for m in (h, heads + h))
    ]
    start_all(kv_in + own_in)

    def own_wait(n):
        return pltpu.make_async_copy(own.at[n], own.at[n], in_sems.at[n + 2])

    if not first:
        carry = [
            pltpu.make_async_copy(a, b, carry_sems.at[n])
            for n, (a, b) in enumerate(zip(carry_in, kept))
        ]
        start_all(carry)

    eye = identity(WIDTH)
    eye_tile = identity(TILE)

    def rows(ref, slot, at, size):
        return ref[slot, at // 32 : (at + size) // 32].reshape(size, WIDTH)

    mine = jnp.int32(0)
    here = lax.axis_index("z") * lax.axis_size("x") + lax.axis_index("x")
    for s in range(owners.shape[0]):
        mine = jnp.where(owners[s] == here, s, mine)
    length = lengths[mine]
    doc_row = docs[pl.ds(mine, 1)]
    start = jnp.zeros_like(doc_row)
    for d in range(8):
        count = jnp.sum((doc_row == d).astype(jnp.int32), axis=1, keepdims=True)
        start = start + jnp.where(doc_row > d, count, 0)
    gain = jnp.broadcast_to(q_gain[...], (TILE, WIDTH)).T
    y, c = my_place()
    if first:
        dk[...] = jnp.zeros_like(dk)
        dv[...] = jnp.zeros_like(dv)
        q_acc[...] = jnp.zeros_like(q_acc)
        wait_all(kv_in)
        for at in range(0, SLOT, TILE):
            part = pl.ds(at, TILE)
            normed = (rms(rows(kv, 0, at, TILE))[0] * k_gain[...]).astype(BF)
            kn[part] = normed
            knt[:, part] = dot_t(eye, normed).astype(BF)
            vt[:, part] = dot_t(eye, rows(kv, 1, at, TILE)).astype(BF)
    else:
        wait_all(kv_in + carry)
    u_rel = lax.broadcasted_iota(jnp.int32, (TILE, TILE), 0)
    t_rel = lax.broadcasted_iota(jnp.int32, (1, TILE), 1)

    def copies_out(n):
        cols = pl.ds(pl.multiple_of(n * WIDTH, WIDTH), WIDTH)
        return [
            pltpu.make_async_copy(
                send.at[lax.rem(y + r // 2, 4), c ^ (r % 2), :, cols], out.at[:, cols], out_sem.at[r]
            )
            for r, out in enumerate(outs)
        ]

    def one_head(h):
        wait_all([own_wait(h), own_wait(heads + h)])
        for group in GROUPS:
            together(h, group)
        start_all(copies_out(h) + copies_out(heads + h))

    def together(h, tiles):
        us = {t: [u for u in range(0, t + 1, TILE) if t - (u + TILE - 1) < REACH] for t in tiles}
        q_inv, q_hat, q_n, g_t, g_b, scores, grads = ({} for _ in range(7))
        for t in tiles:
            q_t = dot_t(eye, rows(own, h, t, TILE))
            g_t[t] = dot_t(eye, rows(own, heads + h, t, TILE))
            g_b[t] = g_t[t].astype(BF)
            q_inv[t] = lax.rsqrt(jnp.mean(q_t * q_t, axis=0, keepdims=True) + EPSILON)
            q_hat[t] = q_t * q_inv[t]
            q_n[t] = (q_hat[t] * gain).astype(BF)
        for t in tiles:
            scores[t] = [dot(kn[pl.ds(u, TILE)], q_n[t]) for u in us[t]]
        for t in tiles:
            grads[t] = [dot(rows(kv, 1, u, TILE), g_b[t]) for u in us[t]]
        largest, weights, factor, probs, low, o_t, delta, dq_t = ({} for _ in range(8))
        for t in tiles:
            first_u = start[:, t : t + TILE]
            for n, u in enumerate(us[t]):
                allowed = u_rel >= first_u - u
                if u == t:
                    allowed = allowed & (u_rel <= t_rel)
                scaled = scores[t][n] * (SCALE * math.log2(math.e))
                scores[t][n] = jnp.where(allowed, scaled, NEG_FILL)
            largest[t] = functools.reduce(
                jnp.maximum, [jnp.max(s, axis=0, keepdims=True) for s in scores[t]]
            )
        for t in tiles:
            weights[t] = [jnp.exp2(s - largest[t]) for s in scores[t]]
            total = sum(jnp.sum(w, axis=0, keepdims=True) for w in weights[t])
            factor[t] = jnp.where(t_rel + t < length, 1.0 / jnp.maximum(total, 1.0), 0.0)
        for t in tiles:
            probs[t] = [w * factor[t] for w in weights[t]]
            low[t] = [p.astype(BF) for p in probs[t]]
            o_t[t] = sum(dot(vt[:, pl.ds(u, TILE)], p) for u, p in zip(us[t], low[t]))
        for t in tiles:
            delta[t] = jnp.sum(g_t[t] * o_t[t], axis=0, keepdims=True)
            for u, p in zip(us[t], low[t]):
                dv[pl.ds(u, TILE)] += dot_t(p, g_b[t])
        for t in tiles:
            dq_t[t] = 0.0
            for u, p, dp in zip(us[t], probs[t], grads[t]):
                part = pl.ds(u, TILE)
                ds = (p * (dp - delta[t])).astype(BF)
                dk[part] += dot_t(ds, q_n[t])
                dq_t[t] += dot(knt[:, part], ds)
        for t in tiles:
            dq = dq_t[t] * SCALE
            q_acc[...] += dq * q_hat[t]
            grad_hat = dq * gain
            inner = jnp.mean(grad_hat * q_hat[t], axis=0, keepdims=True)
            dq = (q_inv[t] * (grad_hat - q_hat[t] * inner)).astype(BF)
            o = dot_t(eye_tile, o_t[t].astype(BF)).astype(BF)
            dq = dot_t(eye_tile, dq).astype(BF)
            for n in range(TILE // WIDTH):
                for to, block in ((h, o), (heads + h, dq)):
                    cols = pl.ds(pl.multiple_of(to * WIDTH, WIDTH), WIDTH)
                    send[t // TILE, n, :, cols] = block[n * WIDTH : (n + 1) * WIDTH]

    def finish():
        k_sum = jnp.zeros((1, WIDTH), F32)
        for at in range(0, SLOT, WIDTH):
            part = pl.ds(at, WIDTH)
            k_hat, k_inv = rms(rows(kv, 0, at, WIDTH))
            gk = dk[part] * SCALE
            k_sum += jnp.sum(gk * k_hat, axis=0, keepdims=True)
            block = at // TILE, at // WIDTH % 2, slice(None)
            grad_k = unnormalize(gk, k_gain[...], k_hat, k_inv).astype(BF)
            send[(*block, column(2 * heads))] = grad_k
            send[(*block, column(2 * heads + 1))] = dv[part].astype(BF)
        start_all(copies_out(2 * heads) + copies_out(2 * heads + 1))
        q_sum = jnp.sum(q_acc[...], axis=1, keepdims=True)
        q_row = jnp.broadcast_to(q_sum, (WIDTH, WIDTH)).T[0:1]
        row = lax.broadcasted_iota(jnp.int32, (SUM_ROWS, WIDTH), 0)
        both = jnp.where(row == 0, q_row, jnp.where(row == 1, k_sum, 0.0))
        sums[...] = jnp.broadcast_to(both, sums.shape)

    if heads == 1:
        one_head(0)
    else:
        pl.loop(0, heads)(one_head)
    if last:
        finish()
    else:
        carry = [
            pltpu.make_async_copy(b, a, carry_sems.at[n])
            for n, (a, b) in enumerate(zip(carry_out, kept))
        ]
        start_all(carry)
        wait_all(carry)
    for r, out in enumerate(outs):
        pltpu.make_async_copy(out, out, out_sem.at[r]).wait()


def place(first_head, heads, last, *refs):
    stage, in_sems, out_sems = refs[-3:]
    received, outs = refs[:8], refs[-7:-3]
    y, c = my_place()
    columns = outs[0].shape[2] // 8
    per = heads * WIDTH
    pieces = [(0, per, 0), (per, per, 1)]
    if last:
        pieces += [(2 * per, WIDTH, 2), (2 * per + WIDTH, WIDTH, 3)]
    loads = [
        pltpu.make_async_copy(ref, stage.at[r], in_sems.at[r]) for r, ref in enumerate(received)
    ]
    start_all(loads)
    stores = []
    for r, load in enumerate(loads):
        load.wait()
        src = lax.rem(y + 4 - r // 2, 4) * 2 + (c ^ (r % 2))
        for n, (at, size, out) in enumerate(pieces):
            start = src * columns + first_head * WIDTH if out < 2 else src * WIDTH
            stores.append(
                pltpu.make_async_copy(
                    stage.at[r, :, pl.ds(at, size)],
                    outs[out].at[0, :, pl.ds(pl.multiple_of(start, WIDTH), size)],
                    out_sems.at[r, n],
                )
            )
            stores[-1].start()
    wait_all(stores)


HBM = pl.BlockSpec(memory_space=pltpu.HBM)
VMEM = pl.BlockSpec(memory_space=pltpu.VMEM)
SMEM = pl.BlockSpec(memory_space=pltpu.SMEM)


def call(kernel, args, in_specs, outs, out_specs, scratch=(), name=None, flops=0, aliases=None):
    moved = sum(math.prod(a.shape) * a.dtype.itemsize for a in (*args, *outs))
    return pl.pallas_call(
        kernel,
        out_shape=outs,
        in_specs=in_specs,
        out_specs=out_specs,
        scratch_shapes=scratch,
        input_output_aliases=aliases or {},
        compiler_params=pltpu.CompilerParams(vmem_limit_bytes=60 * 1024 * 1024),
        cost_estimate=pl.CostEstimate(flops=flops, bytes_accessed=moved, transcendentals=0),
        name=name,
    )(*args)


def shape(dims, dtype=BF):
    return jax.ShapeDtypeStruct(dims, dtype)


def attend_chunk(heads, first, last, owners, lengths, docs, q_gain, k_gain, kv, own, carry):
    args = [owners, lengths, docs, q_gain, k_gain, kv]
    if not first:
        args += [own, *carry]
    width = (2 * heads + (2 if last else 0)) * WIDTH
    outs = [shape((WIDTH, width))] * 8
    kept = [
        ((SLOT, WIDTH), BF),
        ((WIDTH, SLOT), BF),
        ((WIDTH, SLOT), BF),
        ((SLOT, WIDTH), F32),
        ((SLOT, WIDTH), F32),
        ((WIDTH, TILE), F32),
    ]
    per_src = kv.shape[1]
    scratch = [
        pltpu.VMEM((2, SLOT // per_src, per_src, WIDTH), BF),
        pltpu.VMEM((2 * heads, SLOT // per_src, per_src, WIDTH), BF),
        pltpu.VMEM((4, 2, WIDTH, width), BF),
        *(pltpu.VMEM(*a) for a in kept),
        pltpu.SemaphoreType.DMA((2 + 2 * heads,)),
        pltpu.SemaphoreType.DMA((len(kept),)),
        pltpu.SemaphoreType.DMA((8,)),
    ]
    outs += [shape((kv.shape[0], SUM_ROWS, WIDTH), F32)] if last else [shape(*a) for a in kept]
    result = call(
        functools.partial(attend, heads, first, last),
        args,
        [SMEM, SMEM, VMEM, VMEM, VMEM] + [HBM] * (len(args) - 5),
        outs,
        [HBM] * 8 + ([VMEM] if last else [HBM] * len(kept)),
        scratch,
        "attend",
        heads * 12 * 9 * TILE * TILE * WIDTH,
    )
    return result[:8], result[8:]


def across(r):
    return [(i, ((i // 2 + r // 2) % 4) * 2 + ((i % 2) ^ (r % 2))) for i in range(8)]


def packed_chunk(owners, arrays, pieces, by_x):
    seqs, per_src, _ = arrays[0].shape
    width = sum(p[2] for p in pieces)
    count = lax.axis_size("x") if by_x else 1
    block = (seqs // count, per_src, width)
    parts = call(
        functools.partial(pack, pieces),
        [owners, *arrays],
        [SMEM] + [HBM] * len(arrays),
        [shape(block)] * count,
        [HBM] * count,
        [
            pltpu.VMEM((seqs, per_src, width), BF),
            pltpu.SMEM((seqs,), jnp.int32),
            pltpu.SemaphoreType.DMA((4, len(pieces))),
            pltpu.SemaphoreType.DMA((seqs,)),
        ],
        "pack",
    )
    if not by_x:
        return parts[0]
    shift = [[(i, (i + k) % count) for i in range(count)] for k in range(count)]
    parts = [parts[0]] + [lax.ppermute(parts[k], "x", shift[k]) for k in range(1, count)]
    whole = (block[0], count, *block[1:])
    return call(
        regroup,
        parts,
        [HBM] * count,
        [shape(whole)],
        [HBM],
        [pltpu.VMEM(whole, BF), pltpu.SemaphoreType.DMA((count,)), pltpu.SemaphoreType.DMA((1,))],
        "regroup",
    )[0]


def total(spread, axis):
    return jnp.sum(lax.all_to_all(spread, axis, 0, 0, tiled=True), axis=0)


def per_device(query, key, value, grad, q_gain, k_gain, lengths, owners, doc_ids):
    seqs, _, features = query.shape
    heads = features // WIDTH
    head_devs = lax.axis_size("head")
    small = (owners, lengths, doc_ids, q_gain.reshape(1, WIDTH), k_gain.reshape(1, WIDTH))
    chunks, at = [], 0
    for count in CHUNKS:
        width = count * WIDTH
        arrays, pieces = [query, grad], [(at, 0, width), (at, width, width)]
        if at == 0:
            arrays += [key, value]
            pieces += [(0, 2 * width, WIDTH), (0, 2 * width + WIDTH, WIDTH)]
        chunks.append(packed_chunk(owners, arrays, pieces, at > 0))
        at += width
    owned = [lax.all_to_all(chunks[0], DP, 0, 0, tiled=True)]
    received, carry = [], None
    for n, count in enumerate(CHUNKS):
        last = n == len(CHUNKS) - 1
        if not last:
            owned[n], chunk = lax.optimization_barrier((owned[n], chunks[n + 1]))
            owned.append(lax.all_to_all(chunk, "z", 0, 0, tiled=True).reshape(seqs, *query.shape[1:2], -1))
        if n > 0:
            owned[n], received[-1] = lax.optimization_barrier((owned[n], received[-1]))
        out, carry = attend_chunk(count, n == 0, last, *small, owned[0], owned[n], carry)
        received.append([out[0]] + [lax.ppermute(out[r], "head", across(r)) for r in range(1, 8)])
    sums, received[-1][1:4] = lax.optimization_barrier((total(carry[0], DP), received[-1][1:4]))
    sums = total(jnp.broadcast_to(sums, (head_devs, *sums.shape)), "head")
    wide, narrow = shape((1, WIDTH, heads * head_devs * WIDTH)), shape((1, WIDTH, head_devs * WIDTH))
    outs, at = [], 0
    for n, (count, got) in enumerate(zip(CHUNKS, received)):
        outs = call(
            functools.partial(place, at, count, n == len(CHUNKS) - 1),
            [*got, *outs],
            [HBM] * (8 + len(outs)),
            [wide, wide, narrow, narrow],
            [HBM] * 4,
            [
                pltpu.VMEM((8, *got[0].shape), BF),
                pltpu.SemaphoreType.DMA((8,)),
                pltpu.SemaphoreType.DMA((8, 4)),
            ],
            "place",
            aliases={8 + n: n for n in range(4)} if outs else None,
        )
        at += count
    tokens = seqs * SLOT
    return (
        *outs,
        sums[0] / math.sqrt(tokens * heads * head_devs),
        sums[1] / math.sqrt(tokens * head_devs),
    )


def solution(mesh):
    dp, head = mesh.devices.shape
    grid = Mesh(mesh.devices.reshape(dp // 4, 4, head), (*DP, "head"))
    spread = P(None, DP, "head")
    packed = P(DP, "head", None)
    return jax.shard_map(
        per_device,
        mesh=grid,
        in_specs=(spread,) * 4 + (P(),) * 5,
        out_specs=(packed,) * 4 + (P(),) * 2,
        check_vma=False,
    )
```

```python
import functools
import math

import jax
import jax.numpy as jnp
from jax import lax
from jax.experimental import pallas as pl
from jax.experimental.pallas import tpu as pltpu
from jax.sharding import Mesh, PartitionSpec as P

WIDTH = 128
SLOT = 1024
TILE = 256
REACH = 512
CHUNKS = (3, 1)
SUM_ROWS = 16
DP = ("z", "x")
HEAD = ("y", "c")
GROUPS = ((0, 256, 512, 768),)
EPSILON = 1e-06
NEG_FILL = -1e30
SCALE = 1.0 / math.sqrt(WIDTH)
BF = jnp.bfloat16
F32 = jnp.float32


def rms(rows):
    values = rows.astype(F32)
    inverse = lax.rsqrt(jnp.mean(values * values, axis=-1, keepdims=True) + EPSILON)
    return values * inverse, inverse


def unnormalize(grad_normed, gain, normed, inverse):
    grad_hat = grad_normed * gain
    inner = jnp.mean(grad_hat * normed, axis=-1, keepdims=True)
    return inverse * (grad_hat - normed * inner)


def dot(a, b):
    return jnp.dot(a, b, preferred_element_type=F32)


def dot_t(a, b):
    return lax.dot_general(a, b, (((1,), (1,)), ((), ())), preferred_element_type=F32)


def identity(size):
    row = lax.broadcasted_iota(jnp.int32, (size, size), 0)
    col = lax.broadcasted_iota(jnp.int32, (size, size), 1)
    return (row == col).astype(F32).astype(BF)


def start_all(copies):
    for copy in copies:
        copy.start()


def wait_all(copies):
    for copy in copies:
        copy.wait()


def pack(pieces, owners, *refs):
    arrays, refs = refs[: len(pieces)], refs[len(pieces) :]
    *outs, stage, holder, in_sems, out_sems = refs
    seqs = stage.shape[0]
    groups = in_sems.shape[0]
    span = seqs // groups
    loads = [
        [
            pltpu.make_async_copy(
                ref.at[pl.ds(g * span, span), :, pl.ds(at, size)],
                stage.at[pl.ds(g * span, span), :, pl.ds(to, size)],
                in_sems.at[g, n],
            )
            for n, (ref, (at, to, size)) in enumerate(zip(arrays, pieces))
        ]
        for g in range(groups)
    ]
    for group in loads:
        start_all(group)
    if len(outs) == 1:
        for g, group in enumerate(loads):
            wait_all(group)
            for s in range(g * span, (g + 1) * span):
                pltpu.make_async_copy(stage.at[s], outs[0].at[owners[s]], out_sems.at[0]).start()
    else:
        for s in range(seqs):
            holder[owners[s]] = s
        for group in loads:
            wait_all(group)
        for k, out in enumerate(outs):
            x = lax.rem(lax.axis_index("x") + k, len(outs))
            for z in range(out.shape[0]):
                s = holder[z * len(outs) + x]
                pltpu.make_async_copy(stage.at[s], out.at[z], out_sems.at[k]).start()
    for k, out in enumerate(outs):
        pltpu.make_async_copy(out, out, out_sems.at[k]).wait()


def regroup(*refs):
    *arrays, out, stage, in_sems, out_sem = refs
    count = len(arrays)
    loads = []
    for k, ref in enumerate(arrays):
        src = lax.rem(lax.axis_index("x") + count - k, count)
        loads.append(pltpu.make_async_copy(ref, stage.at[:, src], in_sems.at[k]))
    start_all(loads)
    wait_all(loads)
    store = pltpu.make_async_copy(stage, out, out_sem.at[0])
    store.start()
    store.wait()


def my_place():
    return lax.axis_index("y"), lax.axis_index("c")


def attend(heads, first, last, *refs):
    refs = list(refs)
    owners, lengths, docs, q_gain, k_gain, kv_hbm = refs[:6]
    del refs[:6]
    own_hbm = kv_hbm if first else refs.pop(0)
    if not first:
        carry_in = refs[:6]
        del refs[:6]
    outs = refs[:8]
    del refs[:8]
    if last:
        sums = refs.pop(0)
    else:
        carry_out = refs[:6]
        del refs[:6]
    kv, own, send, kn, knt, vt, dk, dv, q_acc, *prior, in_sems, carry_sems, out_sem = refs
    kept = (kn, knt, vt, dk, dv, q_acc)

    def column(n):
        return pl.ds(n * WIDTH, WIDTH)

    base = kv_hbm.shape[2] // WIDTH - 2
    kv_in = [
        pltpu.make_async_copy(kv_hbm.at[:, :, column(base + n)], kv.at[n], in_sems.at[n])
        for n in range(2)
    ]
    own_in = [
        pltpu.make_async_copy(own_hbm.at[:, :, column(n)], own.at[n], in_sems.at[n + 2])
        for n in (m for h in range(heads) for m in (h, heads + h))
    ]
    if first:
        start_all(kv_in + own_in)

    def own_wait(n):
        return pltpu.make_async_copy(own.at[n], own.at[n], in_sems.at[n + 2])

    if not first:
        carry = [
            pltpu.make_async_copy(a, b, carry_sems.at[n])
            for n, (a, b) in enumerate(zip(carry_in, (kn, knt, vt, *prior)))
        ]
        start_all(carry[:1] + own_in[:2] + kv_in[1:] + carry[1:3] + own_in[2:] + kv_in[:1] + carry[3:])

    eye = identity(WIDTH)
    eye_tile = identity(TILE)

    def rows(ref, slot, at, size):
        return ref[slot, at // 32 : (at + size) // 32].reshape(size, WIDTH)

    mine = jnp.int32(0)
    here = lax.axis_index("z") * lax.axis_size("x") + lax.axis_index("x")
    for s in range(owners.shape[0]):
        mine = jnp.where(owners[s] == here, s, mine)
    length = lengths[mine]
    doc_row = docs[pl.ds(mine, 1)]
    start = jnp.zeros_like(doc_row)
    for d in range(8):
        count = jnp.sum((doc_row == d).astype(jnp.int32), axis=1, keepdims=True)
        start = start + jnp.where(doc_row > d, count, 0)
    gain = jnp.broadcast_to(q_gain[...], (TILE, WIDTH)).T
    y, c = my_place()
    dk[...] = jnp.zeros_like(dk)
    dv[...] = jnp.zeros_like(dv)
    q_acc[...] = jnp.zeros_like(q_acc)
    if first:
        wait_all(kv_in)
        for at in range(0, SLOT, TILE):
            part = pl.ds(at, TILE)
            normed = (rms(rows(kv, 0, at, TILE))[0] * k_gain[...]).astype(BF)
            kn[part] = normed
            knt[:, part] = dot_t(eye, normed).astype(BF)
            vt[:, part] = dot_t(eye, rows(kv, 1, at, TILE)).astype(BF)
    else:
        wait_all(kv_in[1:] + carry[:3])
    u_rel = lax.broadcasted_iota(jnp.int32, (TILE, TILE), 0)
    t_rel = lax.broadcasted_iota(jnp.int32, (1, TILE), 1)

    def copies_out(n):
        cols = pl.ds(pl.multiple_of(n * WIDTH, WIDTH), WIDTH)
        return [
            pltpu.make_async_copy(
                send.at[lax.rem(y + r // 2, 4), c ^ (r % 2), :, cols], out.at[:, cols], out_sem.at[r]
            )
            for r, out in enumerate(outs)
        ]

    def one_head(h):
        wait_all([own_wait(h), own_wait(heads + h)])
        for group in GROUPS:
            together(h, group)
        start_all(copies_out(h) + copies_out(heads + h))

    def together(h, tiles):
        us = {t: [u for u in range(0, t + 1, TILE) if t - (u + TILE - 1) < REACH] for t in tiles}
        q_inv, q_hat, q_n, g_t, g_b, scores, grads = ({} for _ in range(7))
        for t in tiles:
            q_t = dot_t(eye, rows(own, h, t, TILE))
            g_t[t] = dot_t(eye, rows(own, heads + h, t, TILE))
            g_b[t] = g_t[t].astype(BF)
            q_inv[t] = lax.rsqrt(jnp.mean(q_t * q_t, axis=0, keepdims=True) + EPSILON)
            q_hat[t] = q_t * q_inv[t]
            q_n[t] = (q_hat[t] * gain).astype(BF)
        for t in tiles:
            scores[t] = [dot(kn[pl.ds(u, TILE)], q_n[t]) for u in us[t]]
        for t in tiles:
            grads[t] = [dot(rows(kv, 1, u, TILE), g_b[t]) for u in us[t]]
        largest, weights, factor, probs, low, o_t, delta, dq_t = ({} for _ in range(8))
        for t in tiles:
            first_u = start[:, t : t + TILE]
            for n, u in enumerate(us[t]):
                allowed = u_rel >= first_u - u
                if u == t:
                    allowed = allowed & (u_rel <= t_rel)
                scaled = scores[t][n] * (SCALE * math.log2(math.e))
                scores[t][n] = jnp.where(allowed, scaled, NEG_FILL)
            largest[t] = functools.reduce(
                jnp.maximum, [jnp.max(s, axis=0, keepdims=True) for s in scores[t]]
            )
        for t in tiles:
            weights[t] = [jnp.exp2(s - largest[t]) for s in scores[t]]
            total = sum(jnp.sum(w, axis=0, keepdims=True) for w in weights[t])
            factor[t] = jnp.where(t_rel + t < length, 1.0 / jnp.maximum(total, 1.0), 0.0)
        for t in tiles:
            probs[t] = [w * factor[t] for w in weights[t]]
            low[t] = [p.astype(BF) for p in probs[t]]
            o_t[t] = sum(dot(vt[:, pl.ds(u, TILE)], p) for u, p in zip(us[t], low[t]))
        for t in tiles:
            delta[t] = jnp.sum(g_t[t] * o_t[t], axis=0, keepdims=True)
            for u, p in zip(us[t], low[t]):
                dv[pl.ds(u, TILE)] += dot_t(p, g_b[t])
        for t in tiles:
            dq_t[t] = 0.0
            for u, p, dp in zip(us[t], probs[t], grads[t]):
                part = pl.ds(u, TILE)
                ds = (p * (dp - delta[t])).astype(BF)
                dk[part] += dot_t(ds, q_n[t])
                dq_t[t] += dot(knt[:, part], ds)
        for t in tiles:
            dq = dq_t[t] * SCALE
            q_acc[...] += dq * q_hat[t]
            grad_hat = dq * gain
            inner = jnp.mean(grad_hat * q_hat[t], axis=0, keepdims=True)
            dq = (q_inv[t] * (grad_hat - q_hat[t] * inner)).astype(BF)
            o = dot_t(eye_tile, o_t[t].astype(BF)).astype(BF)
            dq = dot_t(eye_tile, dq).astype(BF)
            for n in range(TILE // WIDTH):
                for to, block in ((h, o), (heads + h, dq)):
                    cols = pl.ds(pl.multiple_of(to * WIDTH, WIDTH), WIDTH)
                    send[t // TILE, n, :, cols] = block[n * WIDTH : (n + 1) * WIDTH]

    def finish():
        if not first:
            wait_all(kv_in[:1] + carry[3:])
            for ref, before in zip((dk, dv, q_acc), prior):
                ref[...] += before[...]
        k_sum = jnp.zeros((1, WIDTH), F32)
        for at in range(0, SLOT, WIDTH):
            part = pl.ds(at, WIDTH)
            k_hat, k_inv = rms(rows(kv, 0, at, WIDTH))
            gk = dk[part] * SCALE
            k_sum += jnp.sum(gk * k_hat, axis=0, keepdims=True)
            block = at // TILE, at // WIDTH % 2, slice(None)
            grad_k = unnormalize(gk, k_gain[...], k_hat, k_inv).astype(BF)
            send[(*block, column(2 * heads))] = grad_k
            send[(*block, column(2 * heads + 1))] = dv[part].astype(BF)
        start_all(copies_out(2 * heads) + copies_out(2 * heads + 1))
        q_sum = jnp.sum(q_acc[...], axis=1, keepdims=True)
        q_row = jnp.broadcast_to(q_sum, (WIDTH, WIDTH)).T[0:1]
        row = lax.broadcasted_iota(jnp.int32, (SUM_ROWS, WIDTH), 0)
        both = jnp.where(row == 0, q_row, jnp.where(row == 1, k_sum, 0.0))
        sums[...] = jnp.broadcast_to(both, sums.shape)

    if heads == 1:
        one_head(0)
    else:
        pl.loop(0, heads)(one_head)
    if last:
        finish()
    else:
        carry = [
            pltpu.make_async_copy(b, a, carry_sems.at[n])
            for n, (a, b) in enumerate(zip(carry_out, kept))
        ]
        start_all(carry)
        wait_all(carry)
    for r, out in enumerate(outs):
        pltpu.make_async_copy(out, out, out_sem.at[r]).wait()


def place(first_head, heads, last, *refs):
    stage, in_sems, out_sems = refs[-3:]
    received, outs = refs[:8], refs[-7:-3]
    y, c = my_place()
    columns = outs[0].shape[2] // 8
    per = heads * WIDTH
    pieces = [(0, per, 0), (per, per, 1)]
    if last:
        pieces += [(2 * per, WIDTH, 2), (2 * per + WIDTH, WIDTH, 3)]
    loads = [
        pltpu.make_async_copy(ref, stage.at[r], in_sems.at[r]) for r, ref in enumerate(received)
    ]
    start_all(loads)
    stores = []
    for r, load in enumerate(loads):
        load.wait()
        src = lax.rem(y + 4 - r // 2, 4) * 2 + (c ^ (r % 2))
        for n, (at, size, out) in enumerate(pieces):
            start = src * columns + first_head * WIDTH if out < 2 else src * WIDTH
            stores.append(
                pltpu.make_async_copy(
                    stage.at[r, :, pl.ds(at, size)],
                    outs[out].at[0, :, pl.ds(pl.multiple_of(start, WIDTH), size)],
                    out_sems.at[r, n],
                )
            )
            stores[-1].start()
    wait_all(stores)


HBM = pl.BlockSpec(memory_space=pltpu.HBM)
VMEM = pl.BlockSpec(memory_space=pltpu.VMEM)
SMEM = pl.BlockSpec(memory_space=pltpu.SMEM)


def call(kernel, args, in_specs, outs, out_specs, scratch=(), name=None, flops=0, aliases=None):
    moved = sum(math.prod(a.shape) * a.dtype.itemsize for a in (*args, *outs))
    return pl.pallas_call(
        kernel,
        out_shape=outs,
        in_specs=in_specs,
        out_specs=out_specs,
        scratch_shapes=scratch,
        input_output_aliases=aliases or {},
        compiler_params=pltpu.CompilerParams(vmem_limit_bytes=60 * 1024 * 1024),
        cost_estimate=pl.CostEstimate(flops=flops, bytes_accessed=moved, transcendentals=0),
        name=name,
    )(*args)


def shape(dims, dtype=BF):
    return jax.ShapeDtypeStruct(dims, dtype)


def attend_chunk(heads, first, last, owners, lengths, docs, q_gain, k_gain, kv, own, carry):
    args = [owners, lengths, docs, q_gain, k_gain, kv]
    if not first:
        args += [own, *carry]
    width = (2 * heads + (2 if last else 0)) * WIDTH
    outs = [shape((WIDTH, width))] * 8
    kept = [
        ((SLOT, WIDTH), BF),
        ((WIDTH, SLOT), BF),
        ((WIDTH, SLOT), BF),
        ((SLOT, WIDTH), F32),
        ((SLOT, WIDTH), F32),
        ((WIDTH, TILE), F32),
    ]
    per_src = kv.shape[1]
    scratch = [
        pltpu.VMEM((2, SLOT // per_src, per_src, WIDTH), BF),
        pltpu.VMEM((2 * heads, SLOT // per_src, per_src, WIDTH), BF),
        pltpu.VMEM((4, 2, WIDTH, width), BF),
        *(pltpu.VMEM(*a) for a in (kept if first else kept + kept[3:])),
        pltpu.SemaphoreType.DMA((2 + 2 * heads,)),
        pltpu.SemaphoreType.DMA((len(kept),)),
        pltpu.SemaphoreType.DMA((8,)),
    ]
    outs += [shape((16, SUM_ROWS, WIDTH), F32)] if last else [shape(*a) for a in kept]
    result = call(
        functools.partial(attend, heads, first, last),
        args,
        [SMEM, SMEM, VMEM, VMEM, VMEM] + [HBM] * (len(args) - 5),
        outs,
        [HBM] * 8 + ([VMEM] if last else [HBM] * len(kept)),
        scratch,
        "attend",
        heads * 12 * 9 * TILE * TILE * WIDTH,
    )
    return result[:8], result[8:]


def across(r):
    return [(i, ((i // 2 + r // 2) % 4) * 2 + ((i % 2) ^ (r % 2))) for i in range(8)]


def packed_chunk(owners, arrays, pieces, by_x):
    seqs, per_src, _ = arrays[0].shape
    width = sum(p[2] for p in pieces)
    count = lax.axis_size("x") if by_x else 1
    block = (seqs // count, per_src, width)
    parts = call(
        functools.partial(pack, pieces),
        [owners, *arrays],
        [SMEM] + [HBM] * len(arrays),
        [shape(block)] * count,
        [HBM] * count,
        [
            pltpu.VMEM((seqs, per_src, width), BF),
            pltpu.SMEM((seqs,), jnp.int32),
            pltpu.SemaphoreType.DMA((4, len(pieces))),
            pltpu.SemaphoreType.DMA((count,)),
        ],
        "pack",
    )
    if not by_x:
        return parts[0]
    shift = [[(i, (i + k) % count) for i in range(count)] for k in range(count)]
    parts = [parts[0]] + [lax.ppermute(parts[k], "x", shift[k]) for k in range(1, count)]
    whole = (block[0], count, *block[1:])
    return call(
        regroup,
        parts,
        [HBM] * count,
        [shape(whole)],
        [HBM],
        [pltpu.VMEM(whole, BF), pltpu.SemaphoreType.DMA((count,)), pltpu.SemaphoreType.DMA((1,))],
        "regroup",
    )[0]


def total(spread, axis):
    return jnp.sum(lax.all_to_all(spread, axis, 0, 0, tiled=True), axis=0)


def per_device(query, key, value, grad, q_gain, k_gain, lengths, owners, doc_ids):
    seqs, _, features = query.shape
    heads = features // WIDTH
    head_devs = lax.axis_size(HEAD)
    small = (owners, lengths, doc_ids, q_gain.reshape(1, WIDTH), k_gain.reshape(1, WIDTH))
    chunks, at = [], 0
    for count in CHUNKS:
        width = count * WIDTH
        arrays, pieces = [query, grad], [(at, 0, width), (at, width, width)]
        if at == 0:
            arrays += [key, value]
            pieces += [(0, 2 * width, WIDTH), (0, 2 * width + WIDTH, WIDTH)]
        chunks.append(packed_chunk(owners, arrays, pieces, at > 0))
        at += width
    owned = [lax.all_to_all(chunks[0], DP, 0, 0, tiled=True)]
    received, carry = [], None
    for n, count in enumerate(CHUNKS):
        last = n == len(CHUNKS) - 1
        if not last:
            owned[n], chunk = lax.optimization_barrier((owned[n], chunks[n + 1]))
            owned.append(lax.all_to_all(chunk, "z", 0, 0, tiled=True).reshape(seqs, *query.shape[1:2], -1))
        out, carry = attend_chunk(count, n == 0, last, *small, owned[0], owned[n], carry)
        if n > 0:
            out, received[-1] = lax.optimization_barrier((out, received[-1]))
        got = [out[0]] * 8
        for r in (4, 5, 2, 3, 6, 7, 1):
            got[r] = lax.ppermute(out[r], HEAD, across(r))
        received.append(got)
    sums, received[-1][1:2] = lax.optimization_barrier((total(carry[0], ("z", "c")), received[-1][1:2]))
    sums = total(jnp.broadcast_to(sums, carry[0].shape), ("x", "y"))
    wide, narrow = shape((1, WIDTH, heads * head_devs * WIDTH)), shape((1, WIDTH, head_devs * WIDTH))
    outs, at = [], 0
    for n, (count, got) in enumerate(zip(CHUNKS, received)):
        outs = call(
            functools.partial(place, at, count, n == len(CHUNKS) - 1),
            [*got, *outs],
            [HBM] * (8 + len(outs)),
            [wide, wide, narrow, narrow],
            [HBM] * 4,
            [
                pltpu.VMEM((8, *got[0].shape), BF),
                pltpu.SemaphoreType.DMA((8,)),
                pltpu.SemaphoreType.DMA((8, 4)),
            ],
            "place",
            aliases={8 + n: n for n in range(4)} if outs else None,
        )
        at += count
    tokens = seqs * SLOT
    return (
        *outs,
        sums[0] / math.sqrt(tokens * heads * head_devs),
        sums[1] / math.sqrt(tokens * head_devs),
    )


def solution(mesh):
    grid = Mesh(mesh.devices.reshape(8, 4, 4, 2), (*DP, *HEAD))
    spread = P(None, DP, HEAD)
    packed = P(DP, HEAD, None)
    return jax.shard_map(
        per_device,
        mesh=grid,
        in_specs=(spread,) * 4 + (P(),) * 5,
        out_specs=(packed,) * 4 + (P(),) * 2,
        check_vma=False,
    )
```

```python
import functools
import math

import jax
import jax.numpy as jnp
from jax import lax
from jax.experimental import pallas as pl
from jax.experimental.pallas import tpu as pltpu
from jax.sharding import Mesh, PartitionSpec as P

WIDTH = 128
SLOT = 1024
TILE = 256
REACH = 512
CHUNKS = (3, 1)
SUM_ROWS = 16
DP = ("z", "x")
HEAD = ("y", "c")
GROUPS = ((0, 256, 512, 768),)
EPSILON = 1e-06
NEG_FILL = -1e30
SCALE = 1.0 / math.sqrt(WIDTH)
BF = jnp.bfloat16
F32 = jnp.float32


def rms(rows):
    values = rows.astype(F32)
    inverse = lax.rsqrt(jnp.mean(values * values, axis=-1, keepdims=True) + EPSILON)
    return values * inverse, inverse


def unnormalize(grad_normed, gain, normed, inverse):
    grad_hat = grad_normed * gain
    inner = jnp.mean(grad_hat * normed, axis=-1, keepdims=True)
    return inverse * (grad_hat - normed * inner)


def dot(a, b):
    return jnp.dot(a, b, preferred_element_type=F32)


def dot_t(a, b):
    return lax.dot_general(a, b, (((1,), (1,)), ((), ())), preferred_element_type=F32)


def identity(size):
    row = lax.broadcasted_iota(jnp.int32, (size, size), 0)
    col = lax.broadcasted_iota(jnp.int32, (size, size), 1)
    return (row == col).astype(F32).astype(BF)


def start_all(copies):
    for copy in copies:
        copy.start()


def wait_all(copies):
    for copy in copies:
        copy.wait()


def pack(pieces, owners, *refs):
    arrays, refs = refs[: len(pieces)], refs[len(pieces) :]
    *outs, stage, holder, in_sems, out_sems = refs
    seqs = stage.shape[0]
    groups = in_sems.shape[0]
    span = seqs // groups
    loads = [
        [
            pltpu.make_async_copy(
                ref.at[pl.ds(g * span, span), :, pl.ds(at, size)],
                stage.at[pl.ds(g * span, span), :, pl.ds(to, size)],
                in_sems.at[g, n],
            )
            for n, (ref, (at, to, size)) in enumerate(zip(arrays, pieces))
        ]
        for g in range(groups)
    ]
    for group in loads:
        start_all(group)
    if len(outs) == 1:
        for g, group in enumerate(loads):
            wait_all(group)
            for s in range(g * span, (g + 1) * span):
                pltpu.make_async_copy(stage.at[s], outs[0].at[owners[s]], out_sems.at[0]).start()
    else:
        for s in range(seqs):
            holder[owners[s]] = s
        for group in loads:
            wait_all(group)
        for k, out in enumerate(outs):
            x = lax.rem(lax.axis_index("x") + k, len(outs))
            for z in range(out.shape[0]):
                s = holder[z * len(outs) + x]
                pltpu.make_async_copy(stage.at[s], out.at[z], out_sems.at[k]).start()
    for k, out in enumerate(outs):
        pltpu.make_async_copy(out, out, out_sems.at[k]).wait()


def regroup(*refs):
    *arrays, out, stage, in_sems, out_sem = refs
    count = len(arrays)
    loads = []
    for k, ref in enumerate(arrays):
        src = lax.rem(lax.axis_index("x") + count - k, count)
        loads.append(pltpu.make_async_copy(ref, stage.at[:, src], in_sems.at[k]))
    start_all(loads)
    wait_all(loads)
    store = pltpu.make_async_copy(stage, out, out_sem.at[0])
    store.start()
    store.wait()


def my_place():
    return lax.axis_index("y"), lax.axis_index("c")


def attend(heads, first, last, *refs):
    refs = list(refs)
    owners, lengths, docs, q_gain, k_gain, kv_hbm = refs[:6]
    del refs[:6]
    own_hbm = kv_hbm if first else refs.pop(0)
    if not first:
        carry_in = refs[:6]
        del refs[:6]
    outs = refs[:8]
    del refs[:8]
    if last:
        sums = refs.pop(0)
    else:
        carry_out = refs[:6]
        del refs[:6]
    kv, own, send, kn, knt, vt, dk, dv, q_acc, *prior, in_sems, carry_sems, out_sem = refs
    kept = (kn, knt, vt, dk, dv, q_acc)

    def column(n):
        return pl.ds(n * WIDTH, WIDTH)

    base = kv_hbm.shape[2] // WIDTH - 2
    kv_in = [
        pltpu.make_async_copy(kv_hbm.at[:, :, column(base + n)], kv.at[n], in_sems.at[n])
        for n in range(2)
    ]
    own_in = [
        pltpu.make_async_copy(own_hbm.at[:, :, column(n)], own.at[n], in_sems.at[n + 2])
        for n in (m for h in range(heads) for m in (h, heads + h))
    ]
    if first:
        start_all(kv_in + own_in)

    def own_wait(n):
        return pltpu.make_async_copy(own.at[n], own.at[n], in_sems.at[n + 2])

    if not first:
        carry = [
            pltpu.make_async_copy(a, b, carry_sems.at[n])
            for n, (a, b) in enumerate(zip(carry_in, (kn, knt, vt, *prior)))
        ]
        start_all(carry[:1] + own_in[:2] + kv_in[1:] + carry[1:3] + own_in[2:] + kv_in[:1] + carry[3:])

    eye = identity(WIDTH)
    eye_tile = identity(TILE)

    def rows(ref, slot, at, size):
        return ref[slot, at // 32 : (at + size) // 32].reshape(size, WIDTH)

    mine = jnp.int32(0)
    here = lax.axis_index("z") * lax.axis_size("x") + lax.axis_index("x")
    for s in range(owners.shape[0]):
        mine = jnp.where(owners[s] == here, s, mine)
    length = lengths[mine]
    doc_row = docs[pl.ds(mine, 1)]
    start = jnp.zeros_like(doc_row)
    for d in range(8):
        count = jnp.sum((doc_row == d).astype(jnp.int32), axis=1, keepdims=True)
        start = start + jnp.where(doc_row > d, count, 0)
    gain = jnp.broadcast_to(q_gain[...], (TILE, WIDTH)).T
    y, c = my_place()
    dk[...] = jnp.zeros_like(dk)
    dv[...] = jnp.zeros_like(dv)
    q_acc[...] = jnp.zeros_like(q_acc)
    if first:
        wait_all(kv_in + own_in)
        for at in range(0, SLOT, TILE):
            part = pl.ds(at, TILE)
            normed = (rms(rows(kv, 0, at, TILE))[0] * k_gain[...]).astype(BF)
            kn[part] = normed
            knt[:, part] = dot_t(eye, normed).astype(BF)
            vt[:, part] = dot_t(eye, rows(kv, 1, at, TILE)).astype(BF)
    else:
        wait_all(kv_in[1:] + carry[:3] + own_in)
    u_rel = lax.broadcasted_iota(jnp.int32, (TILE, TILE), 0)
    t_rel = lax.broadcasted_iota(jnp.int32, (1, TILE), 1)

    def copies_out(n):
        cols = pl.ds(pl.multiple_of(n * WIDTH, WIDTH), WIDTH)
        return [
            pltpu.make_async_copy(
                send.at[lax.rem(y + r // 2, 4), c ^ (r % 2), :, cols], out.at[:, cols], out_sem.at[r]
            )
            for r, out in enumerate(outs)
        ]

    def one_head(h):
        for group in GROUPS:
            together(h, group)
        start_all(copies_out(h) + copies_out(heads + h))

    def together(h, tiles):
        us = {t: [u for u in range(0, t + 1, TILE) if t - (u + TILE - 1) < REACH] for t in tiles}
        q_inv, q_hat, q_n, g_t, g_b, scores, grads = ({} for _ in range(7))
        for t in tiles:
            q_t = dot_t(eye, rows(own, h, t, TILE))
            g_t[t] = dot_t(eye, rows(own, heads + h, t, TILE))
            g_b[t] = g_t[t].astype(BF)
            q_inv[t] = lax.rsqrt(jnp.mean(q_t * q_t, axis=0, keepdims=True) + EPSILON)
            q_hat[t] = q_t * q_inv[t]
            q_n[t] = (q_hat[t] * gain).astype(BF)
        for t in tiles:
            scores[t] = [dot(kn[pl.ds(u, TILE)], q_n[t]) for u in us[t]]
        for t in tiles:
            grads[t] = [dot(rows(kv, 1, u, TILE), g_b[t]) for u in us[t]]
        largest, weights, factor, probs, low, o_t, delta, dq_t = ({} for _ in range(8))
        for t in tiles:
            first_u = start[:, t : t + TILE]
            for n, u in enumerate(us[t]):
                allowed = u_rel >= first_u - u
                if u == t:
                    allowed = allowed & (u_rel <= t_rel)
                scaled = scores[t][n] * (SCALE * math.log2(math.e))
                scores[t][n] = jnp.where(allowed, scaled, NEG_FILL)
            largest[t] = functools.reduce(
                jnp.maximum, [jnp.max(s, axis=0, keepdims=True) for s in scores[t]]
            )
        for t in tiles:
            weights[t] = [jnp.exp2(s - largest[t]) for s in scores[t]]
            total = sum(jnp.sum(w, axis=0, keepdims=True) for w in weights[t])
            factor[t] = jnp.where(t_rel + t < length, 1.0 / jnp.maximum(total, 1.0), 0.0)
        for t in tiles:
            probs[t] = [w * factor[t] for w in weights[t]]
            low[t] = [p.astype(BF) for p in probs[t]]
            o_t[t] = sum(dot(vt[:, pl.ds(u, TILE)], p) for u, p in zip(us[t], low[t]))
        for t in tiles:
            delta[t] = jnp.sum(g_t[t] * o_t[t], axis=0, keepdims=True)
            for u, p in zip(us[t], low[t]):
                dv[pl.ds(u, TILE)] += dot_t(p, g_b[t])
        for t in tiles:
            dq_t[t] = 0.0
            for u, p, dp in zip(us[t], probs[t], grads[t]):
                part = pl.ds(u, TILE)
                ds = (p * (dp - delta[t])).astype(BF)
                dk[part] += dot_t(ds, q_n[t])
                dq_t[t] += dot(knt[:, part], ds)
        for t in tiles:
            dq = dq_t[t] * SCALE
            q_acc[...] += dq * q_hat[t]
            grad_hat = dq * gain
            inner = jnp.mean(grad_hat * q_hat[t], axis=0, keepdims=True)
            dq = (q_inv[t] * (grad_hat - q_hat[t] * inner)).astype(BF)
            o = dot_t(eye_tile, o_t[t].astype(BF)).astype(BF)
            dq = dot_t(eye_tile, dq).astype(BF)
            for n in range(TILE // WIDTH):
                for to, block in ((h, o), (heads + h, dq)):
                    cols = pl.ds(pl.multiple_of(to * WIDTH, WIDTH), WIDTH)
                    send[t // TILE, n, :, cols] = block[n * WIDTH : (n + 1) * WIDTH]

    def finish():
        if not first:
            wait_all(kv_in[:1] + carry[3:])
            for ref, before in zip((dk, dv, q_acc), prior):
                ref[...] += before[...]
        k_sum = jnp.zeros((1, WIDTH), F32)
        for at in range(0, SLOT, WIDTH):
            part = pl.ds(at, WIDTH)
            k_hat, k_inv = rms(rows(kv, 0, at, WIDTH))
            gk = dk[part] * SCALE
            k_sum += jnp.sum(gk * k_hat, axis=0, keepdims=True)
            block = at // TILE, at // WIDTH % 2, slice(None)
            grad_k = unnormalize(gk, k_gain[...], k_hat, k_inv).astype(BF)
            send[(*block, column(2 * heads))] = grad_k
            send[(*block, column(2 * heads + 1))] = dv[part].astype(BF)
        start_all(copies_out(2 * heads) + copies_out(2 * heads + 1))
        q_sum = jnp.sum(q_acc[...], axis=1, keepdims=True)
        q_row = jnp.broadcast_to(q_sum, (WIDTH, WIDTH)).T[0:1]
        row = lax.broadcasted_iota(jnp.int32, (SUM_ROWS, WIDTH), 0)
        both = jnp.where(row == 0, q_row, jnp.where(row == 1, k_sum, 0.0))
        sums[...] = jnp.broadcast_to(both, sums.shape)

    for h in range(heads):
        one_head(h)
    if last:
        finish()
    else:
        carry = [
            pltpu.make_async_copy(b, a, carry_sems.at[n])
            for n, (a, b) in enumerate(zip(carry_out, kept))
        ]
        start_all(carry)
        wait_all(carry)
    for r, out in enumerate(outs):
        pltpu.make_async_copy(out, out, out_sem.at[r]).wait()


def place(first_head, heads, last, *refs):
    stage, in_sems, out_sems = refs[-3:]
    received, outs = refs[:8], refs[-7:-3]
    y, c = my_place()
    columns = outs[0].shape[2] // 8
    per = heads * WIDTH
    pieces = [(0, per, 0), (per, per, 1)]
    if last:
        pieces += [(2 * per, WIDTH, 2), (2 * per + WIDTH, WIDTH, 3)]
    loads = [
        pltpu.make_async_copy(ref, stage.at[r], in_sems.at[r]) for r, ref in enumerate(received)
    ]
    start_all(loads)
    stores = []
    for r, load in enumerate(loads):
        load.wait()
        src = lax.rem(y + 4 - r // 2, 4) * 2 + (c ^ (r % 2))
        for n, (at, size, out) in enumerate(pieces):
            start = src * columns + first_head * WIDTH if out < 2 else src * WIDTH
            stores.append(
                pltpu.make_async_copy(
                    stage.at[r, :, pl.ds(at, size)],
                    outs[out].at[0, :, pl.ds(pl.multiple_of(start, WIDTH), size)],
                    out_sems.at[r, n],
                )
            )
            stores[-1].start()
    wait_all(stores)


HBM = pl.BlockSpec(memory_space=pltpu.HBM)
VMEM = pl.BlockSpec(memory_space=pltpu.VMEM)
SMEM = pl.BlockSpec(memory_space=pltpu.SMEM)


def call(kernel, args, in_specs, outs, out_specs, scratch=(), name=None, flops=0, aliases=None):
    moved = sum(math.prod(a.shape) * a.dtype.itemsize for a in (*args, *outs))
    return pl.pallas_call(
        kernel,
        out_shape=outs,
        in_specs=in_specs,
        out_specs=out_specs,
        scratch_shapes=scratch,
        input_output_aliases=aliases or {},
        compiler_params=pltpu.CompilerParams(vmem_limit_bytes=60 * 1024 * 1024),
        cost_estimate=pl.CostEstimate(flops=flops, bytes_accessed=moved, transcendentals=0),
        name=name,
    )(*args)


def shape(dims, dtype=BF):
    return jax.ShapeDtypeStruct(dims, dtype)


def attend_chunk(heads, first, last, owners, lengths, docs, q_gain, k_gain, kv, own, carry):
    args = [owners, lengths, docs, q_gain, k_gain, kv]
    if not first:
        args += [own, *carry]
    width = (2 * heads + (2 if last else 0)) * WIDTH
    outs = [shape((WIDTH, width))] * 8
    kept = [
        ((SLOT, WIDTH), BF),
        ((WIDTH, SLOT), BF),
        ((WIDTH, SLOT), BF),
        ((SLOT, WIDTH), F32),
        ((SLOT, WIDTH), F32),
        ((WIDTH, TILE), F32),
    ]
    per_src = kv.shape[1]
    scratch = [
        pltpu.VMEM((2, SLOT // per_src, per_src, WIDTH), BF),
        pltpu.VMEM((2 * heads, SLOT // per_src, per_src, WIDTH), BF),
        pltpu.VMEM((4, 2, WIDTH, width), BF),
        *(pltpu.VMEM(*a) for a in (kept if first else kept + kept[3:])),
        pltpu.SemaphoreType.DMA((2 + 2 * heads,)),
        pltpu.SemaphoreType.DMA((len(kept),)),
        pltpu.SemaphoreType.DMA((8,)),
    ]
    outs += [shape((16, SUM_ROWS, WIDTH), F32)] if last else [shape(*a) for a in kept]
    result = call(
        functools.partial(attend, heads, first, last),
        args,
        [SMEM, SMEM, VMEM, VMEM, VMEM] + [HBM] * (len(args) - 5),
        outs,
        [HBM] * 8 + ([VMEM] if last else [HBM] * len(kept)),
        scratch,
        "attend",
        heads * 12 * 9 * TILE * TILE * WIDTH,
    )
    return result[:8], result[8:]


def across(r):
    return [(i, ((i // 2 + r // 2) % 4) * 2 + ((i % 2) ^ (r % 2))) for i in range(8)]


def packed_chunk(owners, arrays, pieces, by_x):
    seqs, per_src, _ = arrays[0].shape
    width = sum(p[2] for p in pieces)
    count = lax.axis_size("x") if by_x else 1
    block = (seqs // count, per_src, width)
    parts = call(
        functools.partial(pack, pieces),
        [owners, *arrays],
        [SMEM] + [HBM] * len(arrays),
        [shape(block)] * count,
        [HBM] * count,
        [
            pltpu.VMEM((seqs, per_src, width), BF),
            pltpu.SMEM((seqs,), jnp.int32),
            pltpu.SemaphoreType.DMA((4, len(pieces))),
            pltpu.SemaphoreType.DMA((count,)),
        ],
        "pack",
    )
    if not by_x:
        return parts[0]
    shift = [[(i, (i + k) % count) for i in range(count)] for k in range(count)]
    parts = [parts[0]] + [lax.ppermute(parts[k], "x", shift[k]) for k in range(1, count)]
    whole = (block[0], count, *block[1:])
    return call(
        regroup,
        parts,
        [HBM] * count,
        [shape(whole)],
        [HBM],
        [pltpu.VMEM(whole, BF), pltpu.SemaphoreType.DMA((count,)), pltpu.SemaphoreType.DMA((1,))],
        "regroup",
    )[0]


def total(spread, axis):
    return jnp.sum(lax.all_to_all(spread, axis, 0, 0, tiled=True), axis=0)


def per_device(query, key, value, grad, q_gain, k_gain, lengths, owners, doc_ids):
    seqs, _, features = query.shape
    heads = features // WIDTH
    head_devs = lax.axis_size(HEAD)
    small = (owners, lengths, doc_ids, q_gain.reshape(1, WIDTH), k_gain.reshape(1, WIDTH))
    chunks, at = [], 0
    for count in CHUNKS:
        width = count * WIDTH
        arrays, pieces = [query, grad], [(at, 0, width), (at, width, width)]
        if at == 0:
            arrays += [key, value]
            pieces += [(0, 2 * width, WIDTH), (0, 2 * width + WIDTH, WIDTH)]
        chunks.append(packed_chunk(owners, arrays, pieces, at > 0))
        at += width
    owned = [lax.all_to_all(chunks[0], DP, 0, 0, tiled=True)]
    received, carry = [], None
    for n, count in enumerate(CHUNKS):
        last = n == len(CHUNKS) - 1
        if not last:
            owned[n], chunk = lax.optimization_barrier((owned[n], chunks[n + 1]))
            owned.append(lax.all_to_all(chunk, "z", 0, 0, tiled=True).reshape(seqs, *query.shape[1:2], -1))
        out, carry = attend_chunk(count, n == 0, last, *small, owned[0], owned[n], carry)
        if n > 0:
            out, received[-1][2:] = lax.optimization_barrier((out, received[-1][2:]))
        got = [out[0]] * 8
        for r in (4, 5, 2, 3, 6, 7, 1):
            got[r] = lax.ppermute(out[r], HEAD, across(r))
        received.append(got)
    sums = total(carry[0], ("z", "c"))
    sums = total(jnp.broadcast_to(sums, carry[0].shape), ("x", "y"))
    wide, narrow = shape((1, WIDTH, heads * head_devs * WIDTH)), shape((1, WIDTH, head_devs * WIDTH))
    outs, at = [], 0
    for n, (count, got) in enumerate(zip(CHUNKS, received)):
        outs = call(
            functools.partial(place, at, count, n == len(CHUNKS) - 1),
            [*got, *outs],
            [HBM] * (8 + len(outs)),
            [wide, wide, narrow, narrow],
            [HBM] * 4,
            [
                pltpu.VMEM((8, *got[0].shape), BF),
                pltpu.SemaphoreType.DMA((8,)),
                pltpu.SemaphoreType.DMA((8, 4)),
            ],
            "place",
            aliases={8 + n: n for n in range(4)} if outs else None,
        )
        at += count
    tokens = seqs * SLOT
    return (
        *outs,
        sums[0] / math.sqrt(tokens * heads * head_devs),
        sums[1] / math.sqrt(tokens * head_devs),
    )


def solution(mesh):
    grid = Mesh(mesh.devices.reshape(8, 4, 4, 2), (*DP, *HEAD))
    spread = P(None, DP, HEAD)
    packed = P(DP, HEAD, None)
    return jax.shard_map(
        per_device,
        mesh=grid,
        in_specs=(spread,) * 4 + (P(),) * 5,
        out_specs=(packed,) * 4 + (P(),) * 2,
        check_vma=False,
    )
```
